256 devices in a mesh: blk: 8 (over x_lo, y), grp: 32 (over z, x_hi, core).
Axes of the slice: x: 4 (x_hi: 2, x_lo: 2; x = x_hi * 2 + x_lo), y: 4, z: 8, core: 2. Of those that a mesh axis runs over, the one named last changes fastest.
Arguments:
- batch: bfloat16 [1024, 768], P('blk'), may hold values from -6 to 6
- targets: float32 [1024, 512], P('blk'), may hold values from -6 to 6
- centers: bfloat16 [262144, 768], P(('blk', 'grp')), may hold values from -6 to 6
- weights: float32 [262144, 512], P(('blk', 'grp')), may hold values from -32 to 32
- eigvec: float32 [16384, 160], P(('blk', 'grp')), may hold values from -0.375 to 0.375
- eig_scale: float32 [160], replicated, may hold values from 0.05 to 0.95
- step: float32 [1], replicated, may hold values from 122.07031 to 366.21094
Outputs:
- predictions: float32 [1024, 512], P('blk')
- new_weights: float32 [262144, 512], P(('blk', 'grp'))
The draws below stay inside these ranges and needn't reach their ends.
All inputs are finite; a program needn't handle non-finite values.
Results may differ from the reference program's by a relative error of at most 0.00075.
Values may be sent and summed in bfloat16 or wider, within the bound.
No kernel may reach another device: no remote copies, remote signals or barrier semaphores. Data moves between devices by JAX's collectives and lax.ppermute only.
A program may use at most 64 MiB of HBM per device.

```python
import math
import jax
import jax.numpy as jnp
from jax import lax

D = 768
C = 512
CEN_DEV = 1024
NYS_DEV = 64
Q = 160
CENTERS = 262144
BATCH = 1024
NYS = 16384


def shard_levels(rng, extent, shards, least, largest):
    gain = 1.0
    for position, blocks in shards:
        heights = jax.random.uniform(jax.random.fold_in(jax.random.fold_in(rng, 6), position), (blocks,), jnp.float32, least / len(shards), largest / len(shards))
        gain = gain * jnp.repeat(jnp.exp(heights), extent[position] // blocks).reshape((-1,) + (1,) * (len(extent) - 1 - position))
    return gain


def bell_draw(own_key, dims, scale, bound, shards=(), held_as=jnp.bfloat16):
    level = shard_levels(own_key, dims, shards, -0.22, 0.18) if shards else 1.0
    drawn = jax.random.normal(own_key, dims, jnp.float32) * scale * level
    return jnp.minimum(jnp.maximum(drawn, -bound), bound).astype(held_as)


def setup_inputs(seed: int = 0) -> dict:
    keys = jax.random.split(jax.random.key(seed), 8)
    batch = bell_draw(keys[0], (BATCH, D), 1.0, 6.0, ((0, 8),))
    targets = bell_draw(keys[1], (BATCH, C), 1.0, 6.0, ((0, 8),), jnp.float32)
    centers = bell_draw(keys[2], (CENTERS, D), 1.0, 6.0, ((0, 256),))
    weights = bell_draw(keys[3], (CENTERS, C), (2981.0 * CENTERS ** -0.5), 32.0, ((0, 256),), jnp.float32)
    eigvec = bell_draw(keys[4], (NYS, Q), ((NYS * Q) ** -0.25), 0.375, ((0, 256),), jnp.float32)
    eig_scale = jnp.clip(jnp.exp(jax.random.uniform(keys[5], (Q,), jnp.float32, math.log(0.05), math.log(0.95))), 0.05, 0.95)
    step = jnp.clip(jnp.exp(jax.random.uniform(keys[6], (1,), jnp.float32, math.log(122.07031), math.log(366.21094))), 122.07031, 366.21094)
    return dict(batch=batch, targets=targets, centers=centers, weights=weights, eigvec=eigvec, eig_scale=eig_scale, step=step)


def kernel_block(cen, rows):
    cen_sq = jnp.sum(cen.astype(jnp.float32) ** 2, axis=1)
    row_sq = jnp.sum(rows.astype(jnp.float32) ** 2, axis=1)
    cross = jnp.dot(cen, rows.T, preferred_element_type=jnp.float32)
    dist = cen_sq[:, None] + row_sq[None, :] - 2.0 * cross
    return jnp.exp(-dist * (4.0 / cen.shape[1]))


def reference(batch, targets, centers, weights, eigvec, eig_scale, step):
    nblocks = centers.shape[0] // CEN_DEV
    cen_blocks = centers.reshape(nblocks, CEN_DEV, centers.shape[1])
    wgt_blocks = weights.reshape(nblocks, CEN_DEV, weights.shape[1])

    def add_block(total, pair):
        kern = kernel_block(pair[0], batch)
        term = lax.dot_general(kern, pair[1], (((0,), (0,)), ((), ())), precision=lax.Precision.HIGHEST, preferred_element_type=jnp.float32)
        return total + term, None

    start = jnp.zeros((batch.shape[0], weights.shape[1]), jnp.float32)
    predictions, unused = lax.scan(add_block, start, (cen_blocks, wgt_blocks))
    residual = predictions - targets

    def grad_block(cen):
        kern = kernel_block(cen, batch)
        return jnp.dot(kern, residual, precision=lax.Precision.HIGHEST, preferred_element_type=jnp.float32)

    grad = lax.map(grad_block, cen_blocks)
    grad_sub = grad[:, :NYS_DEV].reshape(nblocks * NYS_DEV, weights.shape[1])
    proj = jnp.dot(eigvec.T, grad_sub, precision=lax.Precision.HIGHEST, preferred_element_type=jnp.float32)
    corr = jnp.dot(eigvec, eig_scale[:, None] * proj, precision=lax.Precision.HIGHEST, preferred_element_type=jnp.float32)
    corr = corr.reshape(nblocks, NYS_DEV, weights.shape[1])
    precond = jnp.concatenate([grad[:, :NYS_DEV] - corr, grad[:, NYS_DEV:]], axis=1)
    new_weights = weights - step[0] * precond.reshape(weights.shape)
    return predictions, new_weights
```

```python
import jax
import jax.numpy as jnp
import numpy as np
from jax import lax
from jax.sharding import Mesh, PartitionSpec as P

AXES = ("xl", "y", "z", "xh", "c")
BLK = ("xl", "y")
RING = ("z", "xh")
ALL = P(AXES, None)


def sq_norm(rows):
    return jnp.sum(rows.astype(jnp.float32) ** 2, axis=1)


def kernel_block(cen, cen_sq, rows):
    cross = jnp.dot(cen, rows.T, preferred_element_type=jnp.float32)
    dist = cen_sq[:, None] + sq_norm(rows)[None, :] - 2.0 * cross
    return jnp.exp(-dist * (4.0 / cen.shape[1]))


def contract_rows(a, b, precision=lax.Precision.HIGH):
    return lax.dot_general(
        a, b, (((0,), (0,)), ((), ())), precision=precision, preferred_element_type=jnp.float32
    )


def swap_cores(value):
    return lax.ppermute(value, "c", [(0, 1), (1, 0)])


def spread(value, axes, size):
    return lax.all_to_all(
        jnp.broadcast_to(value[None], (size,) + value.shape), axes, 0, 0, tiled=True
    )


def local(batch, targets, centers, weights, eigvec, eig_scale, step):
    core = lax.axis_index("c")
    slot = lax.axis_index(RING)
    nys = eigvec.shape[0]
    q = eigvec.shape[1]
    c_dim = weights.shape[1]
    half = batch.shape[0] // 2

    own_rows = lax.dynamic_slice_in_dim(batch, core * half, half, 0)
    mine = spread(own_rows, BLK, 8).reshape(8 * half, -1)
    other = swap_cores(mine)
    cen_sq = sq_norm(centers)

    k_other = kernel_block(centers, cen_sq, other)
    k_mine = kernel_block(centers, cen_sq, mine)

    def terms(kern):
        value = contract_rows(kern, weights)
        coef = contract_rows(kern[:nys], eigvec)
        return jnp.concatenate([value, coef], axis=1)

    summed = terms(k_mine) + swap_cores(terms(k_other))
    wide = c_dim + q
    summed = lax.all_to_all(summed.reshape(8, half, wide), BLK, 0, 0, tiled=True).sum(0)
    part = half // 16
    pieces = summed.reshape(16, part, wide)
    pieces = lax.all_to_all(pieces, RING, 0, 0, tiled=True).sum(0)

    whole = spread(pieces, RING, 16).reshape(half, wide)
    own_pred = whole[:, :c_dim]
    other_pred = swap_cores(own_pred)
    predictions = jnp.where(
        core == 0,
        jnp.concatenate([own_pred, other_pred], axis=0),
        jnp.concatenate([other_pred, own_pred], axis=0),
    )
    own_targets = lax.dynamic_slice_in_dim(targets, core * half, half, 0)
    packed = jnp.concatenate([own_pred - own_targets, whole[:, c_dim:]], axis=1).astype(
        jnp.bfloat16
    )
    got_mine = spread(packed, BLK, 8).reshape(8 * half, wide)
    got_other = swap_cores(got_mine)

    scaled = eigvec * eig_scale[None, :]

    def gradient(kern, got):
        resid, coef = got[:, :c_dim], got[:, c_dim:]
        corr = lax.dot_general(
            scaled,
            coef.astype(jnp.float32),
            (((1,), (1,)), ((), ())),
            precision=lax.Precision.HIGH,
            preferred_element_type=jnp.float32,
        )
        kern = jnp.concatenate([kern[:nys] - corr, kern[nys:]], axis=0)
        return jnp.dot(kern.astype(jnp.bfloat16), resid, preferred_element_type=jnp.float32)

    precond = gradient(k_mine, got_mine) + gradient(k_other, got_other)
    new_weights = weights - step[0] * precond
    return (predictions, new_weights)


def solution(mesh):
    fine = Mesh(mesh.devices.reshape(2, 4, 8, 2, 2), AXES)
    return jax.shard_map(
        local,
        mesh=fine,
        in_specs=(P(BLK, None), P(BLK, None), ALL, ALL, ALL, P(), P()),
        out_specs=(P(BLK, None), ALL),
        check_vma=False,
    )
```

```python
import math

import jax
import jax.numpy as jnp
from jax import lax
from jax.experimental import pallas as pl
from jax.experimental.pallas import tpu as pltpu
from jax.sharding import Mesh, PartitionSpec as P

AXES = ("xl", "y", "z", "xh", "c")
BLK = ("xl", "y")
RING = ("z", "xh")
ALL = P(AXES, None)
F32 = jnp.float32
BF16 = jnp.bfloat16
F16 = jnp.float16
NT = (((1,), (1,)), ((), ()))
NN = (((1,), (0,)), ((), ()))

HALF = 64
BLOCKS = 8
LANES = 128
VALUE = 4 * HALF
MAIN = VALUE + HALF
PACKED = MAIN + 16
CODED = PACKED + 16
RING_ROWS = 24
WHOLE = 16 * RING_ROWS
VMEM = 48 * 1024 * 1024


def params():
    return pltpu.CompilerParams(vmem_limit_bytes=VMEM)


def split(value):
    high = value.astype(BF16)
    return high, (value - high.astype(F32)).astype(BF16)


def dot3(a, b, dims):
    a_hi, a_lo = split(a)
    b_hi, b_lo = split(b)

    def one(x, y):
        return lax.dot_general(x, y, dims, preferred_element_type=F32)

    return one(a_hi, b_hi) + one(a_hi, b_lo) + one(a_lo, b_hi)


def lane_group(shape):
    return lax.broadcasted_iota(jnp.int32, shape, len(shape) - 1) // 32


def scale_of(features):
    return 4.0 / features * math.log2(math.e)


def terms_kernel(rows_ref, cen_ref, cs_ref, w_ref, e_ref, out_ref, acc, rs):
    i = pl.program_id(0)
    rows = rows_ref[...]
    scale = scale_of(rows.shape[1])

    @pl.when(i == 0)
    def _():
        wide = rows.astype(F32)
        rs[...] = jnp.sum(wide * wide, axis=1, keepdims=True) * scale
        acc[...] = jnp.zeros_like(acc)

    cross = lax.dot_general(rows, cen_ref[...], NT, preferred_element_type=F32)
    kern = jnp.exp2(cross * (2.0 * scale) - rs[...] - cs_ref[...])
    acc[...] += dot3(kern, w_ref[...], NN)

    @pl.when(i == 0)
    def _():
        coef = dot3(kern[:, :HALF], e_ref[...], NN)
        group = lane_group((16, LANES))
        for b in range(BLOCKS):
            block = coef[b * HALF : (b + 1) * HALF]
            out_ref[b, VALUE:MAIN, :] = block[:, :LANES]
            tail = block[:, LANES:]
            out_ref[b, MAIN:PACKED, :] = jnp.where(
                group < 2,
                jnp.where(group == 0, tail[0:16], tail[16:32]),
                jnp.where(group == 2, tail[32:48], tail[48:64]),
            )

    @pl.when(i == pl.num_programs(0) - 1)
    def _():
        for b in range(BLOCKS):
            for j in range(4):
                out_ref[b, j * HALF : (j + 1) * HALF, :] = acc[
                    b * HALF : (b + 1) * HALF, j * LANES : (j + 1) * LANES
                ]


def terms(rows, centers, cs, weights, eig):
    n, d = rows.shape
    count, c_dim = weights.shape
    tile = 256
    return pl.pallas_call(
        terms_kernel,
        grid=(count // tile,),
        in_specs=[
            pl.BlockSpec((n, d), lambda i: (0, 0)),
            pl.BlockSpec((tile, d), lambda i: (i, 0)),
            pl.BlockSpec((1, tile), lambda i: (0, i)),
            pl.BlockSpec((tile, c_dim), lambda i: (i, 0)),
            pl.BlockSpec(eig.shape, lambda i: (0, 0)),
        ],
        out_specs=pl.BlockSpec((BLOCKS, PACKED, LANES), lambda i: (0, 0, 0)),
        out_shape=jax.ShapeDtypeStruct((BLOCKS, PACKED, LANES), F32),
        scratch_shapes=[pltpu.VMEM((n, c_dim), F32), pltpu.VMEM((n, 1), F32)],
        compiler_params=params(),
        cost_estimate=pl.CostEstimate(
            flops=2 * n * count * (d + 3 * c_dim), bytes_accessed=6 << 20, transcendentals=n * count
        ),
        name="terms",
    )(rows, centers, cs, weights, eig)


def code_kernel(a_ref, b_ref, out_ref):
    for b in range(a_ref.shape[0]):
        total = a_ref[b] + b_ref[b]
        for lo, hi, at in ((0, VALUE, PACKED), (VALUE, PACKED, PACKED + 8)):
            part = total[lo:hi]
            top = jnp.max(jnp.abs(part), axis=(0, 1), keepdims=True)
            power = jnp.ceil(jnp.log2(jnp.maximum(top, 1e-30)))
            out_ref[b, lo:hi, :] = part * jnp.exp2(14.0 - power)
            out_ref[b, at : at + 8, :] = jnp.broadcast_to(power, (8, LANES))


def code(a, b):
    step = 4
    spec = pl.BlockSpec((step, PACKED, LANES), lambda i: (i, 0, 0))
    return pl.pallas_call(
        code_kernel,
        grid=(BLOCKS // step,),
        in_specs=[spec, spec],
        out_specs=pl.BlockSpec((step, CODED, LANES), lambda i: (i, 0, 0)),
        out_shape=jax.ShapeDtypeStruct((BLOCKS, CODED, LANES), F32),
        compiler_params=params(),
        name="code",
    )(a, b)


def decode_kernel(x_ref, out_ref):
    for lo, hi, at in ((0, VALUE, PACKED), (VALUE, PACKED, PACKED + 8)):
        total = jnp.zeros((hi - lo, LANES), F32)
        for b in range(BLOCKS):
            total += x_ref[b, lo:hi, :] * jnp.exp2(x_ref[b, at : at + 1, :] - 14.0)
        out_ref[lo:hi, :] = total
    out_ref[PACKED:WHOLE, :] = jnp.zeros((WHOLE - PACKED, LANES), F32)


def decode(x):
    return pl.pallas_call(
        decode_kernel,
        out_shape=jax.ShapeDtypeStruct((WHOLE, LANES), F32),
        compiler_params=params(),
        name="decode",
    )(x)


def pack_kernel(whole_ref, targets_ref, pred_ref, out_ref):
    for j in range(4):
        lanes = slice(j * LANES, (j + 1) * LANES)
        value = whole_ref[j * HALF : (j + 1) * HALF, :]
        pred_ref[:, lanes] = value
        resid = (value - targets_ref[:, lanes]).astype(BF16)
        for b in range(BLOCKS):
            out_ref[b, j * HALF : (j + 1) * HALF, :] = resid
    coef = whole_ref[VALUE:PACKED, :].astype(BF16)
    for b in range(BLOCKS):
        out_ref[b, VALUE:PACKED, :] = coef


def pack(whole, targets):
    return pl.pallas_call(
        pack_kernel,
        out_shape=(
            jax.ShapeDtypeStruct(targets.shape, F32),
            jax.ShapeDtypeStruct((BLOCKS, PACKED, LANES), BF16),
        ),
        compiler_params=params(),
        name="pack",
    )(whole, targets)


def kern_kernel(cen_ref, first_ref, second_ref, rs_ref, out_ref):
    cen = cen_ref[...]
    scale = scale_of(cen.shape[1])
    wide = cen.astype(F32)
    cs = jnp.sum(wide * wide, axis=1, keepdims=True) * scale
    n = first_ref.shape[0]
    for k, rows_ref in enumerate((first_ref, second_ref)):
        cols = slice(k * n, (k + 1) * n)
        cross = lax.dot_general(cen, rows_ref[...], NT, preferred_element_type=F32)
        out_ref[:, cols] = jnp.exp2(cross * (2.0 * scale) - cs - rs_ref[:, cols]).astype(BF16)


def kern_rows(centers, first, second, rs):
    count, d = centers.shape
    n = first.shape[0]
    tile = 256
    return pl.pallas_call(
        kern_kernel,
        grid=(count // tile,),
        in_specs=[
            pl.BlockSpec((tile, d), lambda i: (i, 0)),
            pl.BlockSpec((n, d), lambda i: (0, 0)),
            pl.BlockSpec((n, d), lambda i: (0, 0)),
            pl.BlockSpec((1, 2 * n), lambda i: (0, 0)),
        ],
        out_specs=pl.BlockSpec((tile, 2 * n), lambda i: (i, 0)),
        out_shape=jax.ShapeDtypeStruct((count, 2 * n), BF16),
        compiler_params=params(),
        cost_estimate=pl.CostEstimate(
            flops=4 * n * count * d, bytes_accessed=5 << 20, transcendentals=2 * n * count
        ),
        name="kern",
    )(centers, first, second, rs)


def step_kernel(step_ref, kern_ref, first_ref, second_ref, eig_ref, w_ref, out_ref, resid, coef):
    i = pl.program_id(0)

    @pl.when(i == 0)
    def _():
        group = lane_group((16, LANES))
        for k, got_ref in enumerate((first_ref, second_ref)):
            for b in range(BLOCKS):
                at = (k * BLOCKS + b) * HALF
                for j in range(4):
                    resid[at : at + HALF, j * LANES : (j + 1) * LANES] = got_ref[
                        b, j * HALF : (j + 1) * HALF, :
                    ]
                coef[at : at + HALF, :LANES] = got_ref[b, VALUE:MAIN, :]
                tail = got_ref[b, MAIN:PACKED, :]
                for t in range(4):
                    coef[at + 16 * t : at + 16 * (t + 1), LANES:] = jnp.where(
                        group == t, tail, jnp.zeros_like(tail)
                    )

    def update(kern):
        grad = lax.dot_general(kern, resid[...], NN, preferred_element_type=F32)
        out_ref[...] = w_ref[...] - step_ref[0] * grad

    @pl.when(i == 0)
    def _():
        e_hi, e_lo = split(eig_ref[...])
        both = coef[...]
        corr = lax.dot_general(e_hi, both, NT, preferred_element_type=F32)
        corr += lax.dot_general(e_lo, both, NT, preferred_element_type=F32)
        kern = kern_ref[...]
        sub = (kern[:HALF].astype(F32) - corr).astype(BF16)
        update(jnp.concatenate([sub, kern[HALF:]], axis=0))

    @pl.when(i > 0)
    def _():
        update(kern_ref[...])


def take_step(step, kern, first, second, eig, weights):
    count, c_dim = weights.shape
    tile = 256
    whole3 = pl.BlockSpec((BLOCKS, PACKED, LANES), lambda i: (0, 0, 0))
    return pl.pallas_call(
        step_kernel,
        grid=(count // tile,),
        in_specs=[
            pl.BlockSpec(memory_space=pltpu.SMEM),
            pl.BlockSpec((tile, kern.shape[1]), lambda i: (i, 0)),
            whole3,
            whole3,
            pl.BlockSpec(eig.shape, lambda i: (0, 0)),
            pl.BlockSpec((tile, c_dim), lambda i: (i, 0)),
        ],
        out_specs=pl.BlockSpec((tile, c_dim), lambda i: (i, 0)),
        out_shape=jax.ShapeDtypeStruct(weights.shape, F32),
        scratch_shapes=[
            pltpu.VMEM((2 * BLOCKS * HALF, c_dim), BF16),
            pltpu.VMEM((2 * BLOCKS * HALF, 2 * LANES), BF16),
        ],
        compiler_params=params(),
        cost_estimate=pl.CostEstimate(
            flops=2 * count * kern.shape[1] * c_dim, bytes_accessed=8 << 20, transcendentals=0
        ),
        name="take_step",
    )(step, kern, first, second, eig, weights)


def sq_norm(rows):
    return jnp.sum(rows.astype(F32) ** 2, axis=1) * scale_of(rows.shape[1])


def swap_cores(value):
    return lax.ppermute(value, "c", [(0, 1), (1, 0)])


def spread(value, axes, size):
    return lax.all_to_all(
        jnp.broadcast_to(value[None], (size,) + value.shape), axes, 0, 0, tiled=True
    )


def wide_eig(eig):
    return jnp.concatenate([eig[:, :LANES]] + [eig[:, LANES:]] * 4, axis=1)


def local(batch, targets, centers, weights, eigvec, eig_scale, step):
    core = lax.axis_index("c")
    d = batch.shape[1]
    cs = sq_norm(centers)[None, :]
    eig = wide_eig(eigvec)
    eig_scaled = wide_eig(eigvec * eig_scale[None, :])

    first = spread(lax.dynamic_slice_in_dim(batch, (1 - core) * HALF, HALF, 0), BLK, BLOCKS)
    first = first.reshape(BLOCKS * HALF, d)
    second = swap_cores(first)
    sent = swap_cores(terms(first, centers, cs, weights, eig))
    coded = code(terms(second, centers, cs, weights, eig), sent)
    coded, first, second = lax.optimization_barrier((coded, first, second))
    got = lax.all_to_all(coded.astype(F16), BLK, 0, 0, tiled=True)

    rs = jnp.concatenate([sq_norm(first), sq_norm(second)])[None, :]
    kern = kern_rows(centers, first, second, rs)

    summed = decode(got.astype(F32)).reshape(16, RING_ROWS, LANES)
    pieces = lax.all_to_all(summed, RING, 0, 0, tiled=True).sum(0)
    whole = spread(pieces, RING, 16).reshape(WHOLE, LANES)

    own_targets = lax.dynamic_slice_in_dim(targets, core * HALF, HALF, 0)
    own_pred, packed = pack(whole, own_targets)
    got_second = lax.all_to_all(packed, BLK, 0, 0, tiled=True)
    got_first = swap_cores(got_second)
    other_pred = swap_cores(own_pred)
    predictions = jnp.where(
        core == 0,
        jnp.concatenate([own_pred, other_pred], axis=0),
        jnp.concatenate([other_pred, own_pred], axis=0),
    )
    new_weights = take_step(step, kern, got_first, got_second, eig_scaled, weights)
    return (predictions, new_weights)


def solution(mesh):
    fine = Mesh(mesh.devices.reshape(2, 4, 8, 2, 2), AXES)
    return jax.shard_map(
        local,
        mesh=fine,
        in_specs=(P(BLK, None), P(BLK, None), ALL, ALL, ALL, P(), P()),
        out_specs=(P(BLK, None), ALL),
        check_vma=False,
    )
```

```python
import math

import jax
import jax.numpy as jnp
from jax import lax
from jax.experimental import pallas as pl
from jax.experimental.pallas import tpu as pltpu
from jax.sharding import Mesh, PartitionSpec as P

AXES = ("xl", "y", "z", "xh", "c")
BLK = ("xl", "y")
RING = ("z", "xh")
ALL = P(AXES, None)
F32 = jnp.float32
BF16 = jnp.bfloat16
F16 = jnp.float16
NT = (((1,), (1,)), ((), ()))
NN = (((1,), (0,)), ((), ()))
TN = (((0,), (0,)), ((), ()))

HALF = 64
BLOCKS = 8
LANES = 128
VALUE = 4 * HALF
MAIN = VALUE + HALF
PACKED = MAIN + 16
CODED = PACKED + 16
RING_ROWS = 24
WHOLE = 16 * RING_ROWS
def params(mib):
    return pltpu.CompilerParams(vmem_limit_bytes=mib << 20)


def split(value):
    high = value.astype(BF16)
    return high, (value - high.astype(F32)).astype(BF16)


def dot3(a, b, dims):
    a_hi, a_lo = split(a)
    b_hi, b_lo = split(b)

    def one(x, y):
        return lax.dot_general(x, y, dims, preferred_element_type=F32)

    return one(a_hi, b_hi) + one(a_hi, b_lo) + one(a_lo, b_hi)


def widen(eig):
    return jnp.concatenate([eig[:, :LANES]] + [eig[:, LANES:]] * 4, axis=1)


def lane_group(shape):
    return lax.broadcasted_iota(jnp.int32, shape, len(shape) - 1) // 32


def scale_of(features):
    return 4.0 / features * math.log2(math.e)


def fan_kernel(core_ref, rows_ref, out_ref):
    rows = rows_ref[...]
    for b in range(BLOCKS):
        out_ref[b] = rows


def fan(batch, core):
    d = batch.shape[1]
    return pl.pallas_call(
        fan_kernel,
        grid_spec=pltpu.PrefetchScalarGridSpec(
            num_scalar_prefetch=1,
            grid=(1,),
            in_specs=[pl.BlockSpec((HALF, d), lambda i, core: (1 - core[0], 0))],
            out_specs=pl.BlockSpec((BLOCKS, HALF, d), lambda i, core: (0, 0, 0)),
        ),
        out_shape=jax.ShapeDtypeStruct((BLOCKS, HALF, d), batch.dtype),
        compiler_params=params(8),
        name="fan",
    )(core, batch)


def weights_kernel(w_ref, out_ref):
    count = w_ref.shape[0]
    high, low = split(w_ref[...])
    out_ref[:count] = high
    out_ref[count : 2 * count] = low
    out_ref[2 * count :] = high


def split_weights(weights):
    count, c_dim = weights.shape
    return pl.pallas_call(
        weights_kernel,
        out_shape=jax.ShapeDtypeStruct((3 * count, c_dim), BF16),
        compiler_params=params(12),
        cost_estimate=pl.CostEstimate(flops=0, bytes_accessed=5 << 20, transcendentals=0),
        name="split_weights",
    )(weights)


def terms_kernel(rows_ref, cen_ref, cs_ref, w_ref, e_ref, out_ref, kern_ref, kern3):
    n, d = rows_ref.shape
    count = cen_ref.shape[0]
    tile = 512
    scale = scale_of(d)
    rows = rows_ref[...]
    wide = rows.astype(F32)
    rs = jnp.sum(wide * wide, axis=1, keepdims=True) * scale
    for at in range(0, count, tile):
        cols = slice(at, at + tile)
        cross = lax.dot_general(rows, cen_ref[cols, :], NT, preferred_element_type=F32)
        kern = jnp.exp2(cross * (2.0 * scale) - rs - cs_ref[:, cols])
        high, low = split(kern)
        kern3[:, at : at + tile] = high
        kern3[:, count + at : count + at + tile] = high
        kern_ref[:, cols] = high
        kern3[:, 2 * count + at : 2 * count + at + tile] = low
        if at == 0:
            coef = dot3(kern[:, :HALF], widen(e_ref[...]), NN)
            group = lane_group((16, LANES))
            for b in range(BLOCKS):
                block = coef[b * HALF : (b + 1) * HALF]
                out_ref[b, VALUE:MAIN, :] = block[:, :LANES]
                tail = block[:, LANES:]
                out_ref[b, MAIN:PACKED, :] = jnp.where(
                    group < 2,
                    jnp.where(group == 0, tail[0:16], tail[16:32]),
                    jnp.where(group == 2, tail[32:48], tail[48:64]),
                )
    value = lax.dot_general(kern3[...], w_ref[...], NN, preferred_element_type=F32)
    for b in range(BLOCKS):
        for j in range(4):
            out_ref[b, j * HALF : (j + 1) * HALF, :] = value[
                b * HALF : (b + 1) * HALF, j * LANES : (j + 1) * LANES
            ]


def terms(rows, centers, cs, weights3, eig):
    n, d = rows.shape
    count = centers.shape[0]
    c_dim = weights3.shape[1]
    return pl.pallas_call(
        terms_kernel,
        out_shape=(
            jax.ShapeDtypeStruct((BLOCKS, PACKED, LANES), F32),
            jax.ShapeDtypeStruct((n, count), BF16),
        ),
        scratch_shapes=[pltpu.VMEM((n, 3 * count), BF16)],
        compiler_params=params(24),
        cost_estimate=pl.CostEstimate(
            flops=20 * n * count * (d + 3 * c_dim), bytes_accessed=6 << 20, transcendentals=n * count
        ),
        name="terms",
    )(rows, centers, cs, weights3, eig)


def code_kernel(a_ref, b_ref, out_ref):
    for b in range(a_ref.shape[0]):
        total = a_ref[b] + b_ref[b]
        for lo, hi, at in ((0, VALUE, PACKED), (VALUE, PACKED, PACKED + 8)):
            part = total[lo:hi]
            top = jnp.max(jnp.abs(part), axis=(0, 1), keepdims=True)
            power = jnp.ceil(jnp.log2(jnp.maximum(top, 1e-30)))
            out_ref[b, lo:hi, :] = part * jnp.exp2(14.0 - power)
            out_ref[b, at : at + 8, :] = jnp.broadcast_to(power, (8, LANES))


def code(a, b):
    step = 4
    spec = pl.BlockSpec((step, PACKED, LANES), lambda i: (i, 0, 0))
    return pl.pallas_call(
        code_kernel,
        grid=(BLOCKS // step,),
        in_specs=[spec, spec],
        out_specs=pl.BlockSpec((step, CODED, LANES), lambda i: (i, 0, 0)),
        out_shape=jax.ShapeDtypeStruct((BLOCKS, CODED, LANES), F32),
        compiler_params=params(12),
        name="code",
    )(a, b)


def decode_kernel(x_ref, out_ref):
    for lo, hi, at in ((0, VALUE, PACKED), (VALUE, PACKED, PACKED + 8)):
        total = jnp.zeros((hi - lo, LANES), F32)
        for b in range(BLOCKS):
            total += x_ref[b, lo:hi, :] * jnp.exp2(x_ref[b, at : at + 1, :] - 14.0)
        out_ref[lo:hi, :] = total
    out_ref[PACKED:WHOLE, :] = jnp.zeros((WHOLE - PACKED, LANES), F32)


def decode(x):
    return pl.pallas_call(
        decode_kernel,
        out_shape=jax.ShapeDtypeStruct((WHOLE, LANES), F32),
        compiler_params=params(12),
        name="decode",
    )(x)


def pack_kernel(core_ref, whole_ref, targets_ref, pred_ref, out_ref):
    for j in range(4):
        lanes = slice(j * LANES, (j + 1) * LANES)
        value = whole_ref[j * HALF : (j + 1) * HALF, :]
        pred_ref[:, lanes] = value
        resid = (value - targets_ref[:, lanes]).astype(BF16)
        for b in range(BLOCKS):
            out_ref[b, j * HALF : (j + 1) * HALF, :] = resid
    coef = whole_ref[VALUE:PACKED, :].astype(BF16)
    for b in range(BLOCKS):
        out_ref[b, VALUE:PACKED, :] = coef


def pack(whole, targets, core):
    c_dim = targets.shape[1]
    return pl.pallas_call(
        pack_kernel,
        grid_spec=pltpu.PrefetchScalarGridSpec(
            num_scalar_prefetch=1,
            grid=(1,),
            in_specs=[
                pl.BlockSpec((WHOLE, LANES), lambda i, core: (0, 0)),
                pl.BlockSpec((HALF, c_dim), lambda i, core: (core[0], 0)),
            ],
            out_specs=(
                pl.BlockSpec((HALF, c_dim), lambda i, core: (0, 0)),
                pl.BlockSpec((BLOCKS, PACKED, LANES), lambda i, core: (0, 0, 0)),
            ),
        ),
        out_shape=(
            jax.ShapeDtypeStruct((HALF, c_dim), F32),
            jax.ShapeDtypeStruct((BLOCKS, PACKED, LANES), BF16),
        ),
        compiler_params=params(8),
        name="pack",
    )(core, whole, targets)


def gradient(kern_ref, got_ref, eig_ref, scale_ref, resid, head, tile, add):
    count = kern_ref.shape[1]
    group = lane_group((16, LANES))
    coefs = []
    for b in range(BLOCKS):
        at = b * HALF
        for j in range(4):
            resid[at : at + HALF, j * LANES : (j + 1) * LANES] = got_ref[
                b, j * HALF : (j + 1) * HALF, :
            ]
        tail = got_ref[b, MAIN:PACKED, :]
        zero = jnp.zeros_like(tail)
        tails = [jnp.where(group == t, tail, zero) for t in range(4)]
        coefs.append(
            jnp.concatenate(
                [got_ref[b, VALUE:MAIN, :], jnp.concatenate(tails, axis=0)], axis=1
            )
        )
    coef = jnp.concatenate(coefs, axis=0)
    corr = jnp.zeros((coef.shape[0], HALF), F32)
    for part in split(widen(eig_ref[...] * scale_ref[...])):
        corr += lax.dot_general(coef, part, NT, preferred_element_type=F32)
    head[...] = kern_ref[:, :LANES]
    head[:, :HALF] = (kern_ref[:, :HALF].astype(F32) - corr).astype(BF16)
    for at in range(0, count, tile):
        if at == 0:
            kern = jnp.concatenate([head[...], kern_ref[:, LANES:tile]], axis=1)
        else:
            kern = kern_ref[:, at : at + tile]
        add(
            slice(at, at + tile),
            lax.dot_general(kern, resid[...], TN, preferred_element_type=F32),
        )


def half_kernel(kern_ref, got_ref, eig_ref, scale_ref, out_ref, resid, head):
    def add(rows, product):
        out_ref[rows, :] = product

    gradient(kern_ref, got_ref, eig_ref, scale_ref, resid, head, 512, add)


def half_scratch(n, c_dim):
    return [pltpu.VMEM((n, c_dim), BF16), pltpu.VMEM((n, LANES), BF16)]


def half_gradient(kern, got, eig, scale, c_dim):
    n, count = kern.shape
    return pl.pallas_call(
        half_kernel,
        out_shape=jax.ShapeDtypeStruct((count, c_dim), F32),
        scratch_shapes=half_scratch(n, c_dim),
        compiler_params=params(16),
        cost_estimate=pl.CostEstimate(
            flops=20 * n * count * c_dim, bytes_accessed=4 << 20, transcendentals=0
        ),
        name="half_gradient",
    )(kern, got, eig, scale)


def step_kernel(
    step_ref,
    core_ref,
    kern_ref,
    got_ref,
    eig_ref,
    scale_ref,
    grad_ref,
    w_ref,
    own_ref,
    other_ref,
    pred_ref,
    out_ref,
    resid,
    head,
    new,
    sem,
    pred_sem,
):
    step = step_ref[0]
    core = core_ref[0]
    copies = []
    own_copy = pltpu.make_async_copy(
        own_ref, pred_ref.at[pl.ds(pl.multiple_of(core * HALF, HALF), HALF)], pred_sem.at[0]
    )
    other_copy = pltpu.make_async_copy(
        other_ref,
        pred_ref.at[pl.ds(pl.multiple_of((1 - core) * HALF, HALF), HALF)],
        pred_sem.at[1],
    )
    own_copy.start()
    other_copy.start()

    def add(rows, product):
        new[rows, :] = w_ref[rows, :] - step * (grad_ref[rows, :] + product)
        k = len(copies)
        copies.append(pltpu.make_async_copy(new.at[rows], out_ref.at[rows], sem.at[k]))
        copies[k].start()

    gradient(kern_ref, got_ref, eig_ref, scale_ref, resid, head, 256, add)
    own_copy.wait()
    other_copy.wait()
    for copy in copies:
        copy.wait()


def take_step(step, core, kern, got, eig, scale, grad, weights, own, other):
    n, count = kern.shape
    c_dim = weights.shape[1]
    smem = pl.BlockSpec(memory_space=pltpu.SMEM)
    vmem = pl.BlockSpec(memory_space=pltpu.VMEM)
    return pl.pallas_call(
        step_kernel,
        in_specs=[smem] * 2 + [vmem] * 8,
        out_specs=[pl.BlockSpec(memory_space=pltpu.HBM)] * 2,
        out_shape=(
            jax.ShapeDtypeStruct((2 * HALF, c_dim), F32),
            jax.ShapeDtypeStruct(weights.shape, F32),
        ),
        scratch_shapes=half_scratch(n, c_dim)
        + [
            pltpu.VMEM(weights.shape, F32),
            pltpu.SemaphoreType.DMA((4,)),
            pltpu.SemaphoreType.DMA((2,)),
        ],
        compiler_params=params(16),
        cost_estimate=pl.CostEstimate(
            flops=2 * n * count * c_dim, bytes_accessed=8 << 20, transcendentals=0
        ),
        name="take_step",
    )(step, core, kern, got, eig, scale, grad, weights, own, other)


def sq_norm(rows):
    return jnp.sum(rows.astype(F32) ** 2, axis=1) * scale_of(rows.shape[1])


def swap_cores(value):
    return lax.ppermute(value, "c", [(0, 1), (1, 0)])


def spread(value, axes, size):
    return lax.all_to_all(
        jnp.broadcast_to(value[None], (size,) + value.shape), axes, 0, 0, tiled=True
    )


def local(batch, targets, centers, weights, eigvec, eig_scale, step):
    core = lax.axis_index("c")
    half = core.reshape(1)
    n, d = BLOCKS * HALF, batch.shape[1]
    c_dim = weights.shape[1]

    first = lax.all_to_all(fan(batch, half), BLK, 0, 0, tiled=True).reshape(n, d)
    first, held, to_split = lax.optimization_barrier((first, centers, weights))
    second = swap_cores(first)
    cs = sq_norm(held)[None, :]
    weights3 = split_weights(to_split)
    sent, kern_first = terms(first, held, cs, weights3, eigvec)
    kept, kern_second = terms(second, held, cs, weights3, eigvec)
    coded = code(kept, swap_cores(sent)).astype(F16)

    got = lax.all_to_all(coded, BLK, 0, 0, tiled=True)
    summed = decode(got.astype(F32)).reshape(16, RING_ROWS, LANES)
    pieces = lax.all_to_all(summed, RING, 0, 0, tiled=True).sum(0)
    whole = spread(pieces, RING, 16).reshape(WHOLE, LANES)

    own_pred, packed = pack(whole, targets, half)
    got_second = lax.all_to_all(packed, BLK, 0, 0, tiled=True)
    got_second, own_pred = lax.optimization_barrier((got_second, own_pred))
    got_first = swap_cores(got_second)
    other_pred = swap_cores(own_pred)
    scale = eig_scale[None, :]
    grad = half_gradient(kern_second, got_second, eigvec, scale, c_dim)
    return take_step(
        step, half, kern_first, got_first, eigvec, scale, grad, weights, own_pred, other_pred
    )


def solution(mesh):
    fine = Mesh(mesh.devices.reshape(2, 4, 8, 2, 2), AXES)
    return jax.shard_map(
        local,
        mesh=fine,
        in_specs=(P(BLK, None), P(BLK, None), ALL, ALL, ALL, P(), P()),
        out_specs=(P(BLK, None), ALL),
        check_vma=False,
    )
```

```python
import math

import jax
import jax.numpy as jnp
from jax import lax
from jax.experimental import pallas as pl
from jax.experimental.pallas import tpu as pltpu
from jax.sharding import Mesh, PartitionSpec as P

AXES = ("xl", "y", "z", "xh", "c")
BLK = ("xl", "y")
PLANE = ("xl", "y", "xh")
RING = ("xh", "z")
ALL = P(AXES, None)
F32 = jnp.float32
BF16 = jnp.bfloat16
F16 = jnp.float16
NT = (((1,), (1,)), ((), ()))
NN = (((1,), (0,)), ((), ()))
TN = (((0,), (0,)), ((), ()))

HALF = 64
BLOCKS = 8
SUB = 32
SUBS = 16
LANES = 128
VALUE = 4 * SUB
MAIN = VALUE + SUB
PACKED = MAIN + 8
CODED = PACKED + 8
RING_ROWS = 24
RING_SIZE = 8
WHOLE = RING_SIZE * RING_ROWS
BACK_VALUE = 2 * VALUE
BACK_MAIN = 2 * MAIN
BACK = 2 * PACKED


def params(mib):
    return pltpu.CompilerParams(vmem_limit_bytes=mib << 20)


def split(value):
    high = value.astype(BF16)
    return high, (value - high.astype(F32)).astype(BF16)


def dot3(a, b, dims):
    a_hi, a_lo = split(a)
    b_hi, b_lo = split(b)

    def one(x, y):
        return lax.dot_general(x, y, dims, preferred_element_type=F32)

    return one(a_hi, b_hi) + one(a_hi, b_lo) + one(a_lo, b_hi)


def widen(eig):
    return jnp.concatenate([eig[:, :LANES]] + [eig[:, LANES:]] * 4, axis=1)


def lane_group(shape):
    return lax.broadcasted_iota(jnp.int32, shape, len(shape) - 1) // 32


def scale_of(features):
    return 4.0 / features * math.log2(math.e)


def fan_kernel(core_ref, rows_ref, out_ref):
    rows = rows_ref[...]
    for b in range(BLOCKS):
        out_ref[b] = rows


def fan(core, batch):
    d = batch.shape[1]
    return pl.pallas_call(
        fan_kernel,
        grid_spec=pltpu.PrefetchScalarGridSpec(
            num_scalar_prefetch=1,
            grid=(1,),
            in_specs=[pl.BlockSpec((HALF, d), lambda i, core: (1 - core[0], 0))],
            out_specs=pl.BlockSpec((BLOCKS, HALF, d), lambda i, core: (0, 0, 0)),
        ),
        out_shape=jax.ShapeDtypeStruct((BLOCKS, HALF, d), batch.dtype),
        compiler_params=params(8),
        name="fan",
    )(core, batch)


def weights_kernel(w_ref, out_ref):
    count = w_ref.shape[0]
    high, low = split(w_ref[...])
    out_ref[:count] = high
    out_ref[count : 2 * count] = low
    out_ref[2 * count :] = high


def split_weights(weights):
    count, c_dim = weights.shape
    return pl.pallas_call(
        weights_kernel,
        out_shape=jax.ShapeDtypeStruct((3 * count, c_dim), BF16),
        compiler_params=params(12),
        cost_estimate=pl.CostEstimate(flops=0, bytes_accessed=5 << 20, transcendentals=0),
        name="split_weights",
    )(weights)


def terms_kernel(rows_ref, cen_ref, cs_ref, w_ref, e_ref, out_ref, kern_ref, kern3):
    n, d = rows_ref.shape
    count = cen_ref.shape[0]
    tile = 512
    scale = scale_of(d)
    rows = rows_ref[...]
    wide = rows.astype(F32)
    rs = jnp.sum(wide * wide, axis=1, keepdims=True) * scale
    for at in range(0, count, tile):
        cols = slice(at, at + tile)
        cross = lax.dot_general(rows, cen_ref[cols, :], NT, preferred_element_type=F32)
        kern = jnp.exp2(cross * (2.0 * scale) - rs - cs_ref[:, cols])
        high, low = split(kern)
        kern3[:, at : at + tile] = high
        kern3[:, count + at : count + at + tile] = high
        kern_ref[:, cols] = high
        kern3[:, 2 * count + at : 2 * count + at + tile] = low
        if at == 0:
            coef = dot3(kern[:, :HALF], widen(e_ref[...]), NN)
            group = lane_group((8, LANES))
            for b in range(SUBS):
                block = coef[b * SUB : (b + 1) * SUB]
                out_ref[b, VALUE:MAIN, :] = block[:, :LANES]
                tail = block[:, LANES:]
                out_ref[b, MAIN:PACKED, :] = jnp.where(
                    group < 2,
                    jnp.where(group == 0, tail[0:8], tail[8:16]),
                    jnp.where(group == 2, tail[16:24], tail[24:32]),
                )
    value = lax.dot_general(kern3[...], w_ref[...], NN, preferred_element_type=F32)
    for b in range(SUBS):
        for j in range(4):
            out_ref[b, j * SUB : (j + 1) * SUB, :] = value[
                b * SUB : (b + 1) * SUB, j * LANES : (j + 1) * LANES
            ]


def terms(rows, centers, cs, weights3, eig):
    n, d = rows.shape
    count = centers.shape[0]
    c_dim = weights3.shape[1]
    return pl.pallas_call(
        terms_kernel,
        out_shape=(
            jax.ShapeDtypeStruct((SUBS, PACKED, LANES), F32),
            jax.ShapeDtypeStruct((n, count), BF16),
        ),
        scratch_shapes=[pltpu.VMEM((n, 3 * count), BF16)],
        compiler_params=params(24),
        cost_estimate=pl.CostEstimate(
            flops=20 * n * count * (d + 3 * c_dim), bytes_accessed=6 << 20, transcendentals=n * count
        ),
        name="terms",
    )(rows, centers, cs, weights3, eig)


def code_kernel(a_ref, b_ref, out_ref):
    upper = lax.broadcasted_iota(jnp.int32, (8, LANES), 0) < 4
    for b in range(a_ref.shape[0]):
        total = a_ref[b] + b_ref[b]
        powers = []
        for lo, hi in ((0, VALUE), (VALUE, PACKED)):
            part = total[lo:hi]
            top = jnp.max(jnp.abs(part), axis=(0, 1), keepdims=True)
            power = jnp.ceil(jnp.log2(jnp.maximum(top, 1e-30)))
            out_ref[b, lo:hi, :] = part * jnp.exp2(14.0 - power)
            powers.append(jnp.broadcast_to(power, (8, LANES)))
        out_ref[b, PACKED:CODED, :] = jnp.where(upper, powers[0], powers[1])


def code(a, b):
    step = 8
    spec = pl.BlockSpec((step, PACKED, LANES), lambda i: (i, 0, 0))
    return pl.pallas_call(
        code_kernel,
        grid=(SUBS // step,),
        in_specs=[spec, spec],
        out_specs=pl.BlockSpec((step, CODED, LANES), lambda i: (i, 0, 0)),
        out_shape=jax.ShapeDtypeStruct((SUBS, CODED, LANES), F32),
        compiler_params=params(12),
        name="code",
    )(a, b)


def decode_kernel(x_ref, out_ref):
    for lo, hi, at in ((0, VALUE, PACKED), (VALUE, PACKED, PACKED + 4)):
        total = jnp.zeros((hi - lo, LANES), F32)
        for b in range(SUBS):
            total += x_ref[b, lo:hi, :] * jnp.exp2(x_ref[b, at : at + 1, :] - 14.0)
        out_ref[lo:hi, :] = total
    out_ref[PACKED:WHOLE, :] = jnp.zeros((WHOLE - PACKED, LANES), F32)


def decode(x):
    return pl.pallas_call(
        decode_kernel,
        out_shape=jax.ShapeDtypeStruct((WHOLE, LANES), F32),
        compiler_params=params(12),
        name="decode",
    )(x)


def ring_kernel(x_ref, out_ref):
    total = x_ref[0]
    for z in range(1, RING_SIZE):
        total += x_ref[z]
    for k in range(2 * RING_SIZE):
        out_ref[k] = total


def ring_fan(x):
    return pl.pallas_call(
        ring_kernel,
        out_shape=jax.ShapeDtypeStruct((2 * RING_SIZE, RING_ROWS, LANES), F32),
        compiler_params=params(8),
        name="ring_fan",
    )(x)


def pack_kernel(core_ref, whole_ref, targets_ref, pred_ref, out_ref):
    for h in range(2):
        rows = slice(h * SUB, (h + 1) * SUB)
        for j in range(4):
            lanes = slice(j * LANES, (j + 1) * LANES)
            value = whole_ref[h, j * SUB : (j + 1) * SUB, :]
            pred_ref[rows, lanes] = value
            resid = (value - targets_ref[rows, lanes]).astype(BF16)
            at = j * HALF + h * SUB
            for b in range(BLOCKS):
                out_ref[b, at : at + SUB, :] = resid
        coef = whole_ref[h, VALUE:MAIN, :].astype(BF16)
        at = BACK_VALUE + h * SUB
        for b in range(BLOCKS):
            out_ref[b, at : at + SUB, :] = coef
    tails = [whole_ref[h, MAIN:PACKED, :] for h in range(2)]
    tail = jnp.concatenate(tails, axis=0).astype(BF16)
    for b in range(BLOCKS):
        out_ref[b, BACK_MAIN:BACK, :] = tail


def pack(whole, targets, core):
    c_dim = targets.shape[1]
    return pl.pallas_call(
        pack_kernel,
        grid_spec=pltpu.PrefetchScalarGridSpec(
            num_scalar_prefetch=1,
            grid=(1,),
            in_specs=[
                pl.BlockSpec((2, WHOLE, LANES), lambda i, core: (0, 0, 0)),
                pl.BlockSpec((HALF, c_dim), lambda i, core: (core[0], 0)),
            ],
            out_specs=(
                pl.BlockSpec((HALF, c_dim), lambda i, core: (0, 0)),
                pl.BlockSpec((BLOCKS, BACK, LANES), lambda i, core: (0, 0, 0)),
            ),
        ),
        out_shape=(
            jax.ShapeDtypeStruct((HALF, c_dim), F32),
            jax.ShapeDtypeStruct((BLOCKS, BACK, LANES), BF16),
        ),
        compiler_params=params(8),
        name="pack",
    )(core, whole, targets)


def gradient(kern_ref, got_ref, eig_ref, scale_ref, resid, head, tile, add):
    count = kern_ref.shape[1]
    group = lane_group((8, LANES))
    coefs = []
    for b in range(BLOCKS):
        at = b * HALF
        for j in range(4):
            resid[at : at + HALF, j * LANES : (j + 1) * LANES] = got_ref[
                b, j * HALF : (j + 1) * HALF, :
            ]
        tail = got_ref[b, BACK_MAIN:BACK, :].astype(F32)
        tails = [
            jnp.where(group == t, tail[8 * h : 8 * h + 8], 0.0) for h in range(2) for t in range(4)
        ]
        coefs.append(
            jnp.concatenate(
                [got_ref[b, BACK_VALUE:BACK_MAIN, :], jnp.concatenate(tails, axis=0).astype(BF16)],
                axis=1,
            )
        )
    coef = jnp.concatenate(coefs, axis=0)
    corr = jnp.zeros((coef.shape[0], HALF), F32)
    for part in split(widen(eig_ref[...] * scale_ref[...])):
        corr += lax.dot_general(coef, part, NT, preferred_element_type=F32)
    head[...] = kern_ref[:, :LANES]
    head[:, :HALF] = (kern_ref[:, :HALF].astype(F32) - corr).astype(BF16)
    for at in range(0, count, tile):
        if at == 0:
            kern = jnp.concatenate([head[...], kern_ref[:, LANES:tile]], axis=1)
        else:
            kern = kern_ref[:, at : at + tile]
        add(
            slice(at, at + tile),
            lax.dot_general(kern, resid[...], TN, preferred_element_type=F32),
        )


def gradient_scratch(n, c_dim):
    return [pltpu.VMEM((n, c_dim), BF16), pltpu.VMEM((n, LANES), BF16)]


def half_kernel(kern_ref, got_ref, eig_ref, scale_ref, out_ref, resid, head):
    def add(rows, product):
        out_ref[rows, :] = product

    gradient(kern_ref, got_ref, eig_ref, scale_ref, resid, head, 512, add)


def half_gradient(kern, got, eig, scale, c_dim):
    n, count = kern.shape
    return pl.pallas_call(
        half_kernel,
        out_shape=jax.ShapeDtypeStruct((count, c_dim), F32),
        scratch_shapes=gradient_scratch(n, c_dim),
        compiler_params=params(16),
        cost_estimate=pl.CostEstimate(
            flops=20 * n * count * c_dim, bytes_accessed=4 << 20, transcendentals=0
        ),
        name="half_gradient",
    )(kern, got, eig, scale)


def step_kernel(
    core_ref,
    kern_ref,
    got_ref,
    eig_ref,
    scale_ref,
    step_ref,
    grad_ref,
    w_ref,
    own_ref,
    other_ref,
    pred_ref,
    out_ref,
    resid,
    head,
    new,
    sem,
    pred_sem,
):
    core = core_ref[0]
    own_copy = pltpu.make_async_copy(
        own_ref, pred_ref.at[pl.ds(pl.multiple_of(core * HALF, HALF), HALF)], pred_sem.at[0]
    )
    other_copy = pltpu.make_async_copy(
        other_ref,
        pred_ref.at[pl.ds(pl.multiple_of((1 - core) * HALF, HALF), HALF)],
        pred_sem.at[1],
    )
    own_copy.start()
    other_copy.start()
    step = step_ref[...]
    copies = []

    def add(rows, product):
        new[rows, :] = w_ref[rows, :] - step * (grad_ref[rows, :] + product)
        k = len(copies)
        copies.append(pltpu.make_async_copy(new.at[rows], out_ref.at[rows], sem.at[k]))
        copies[k].start()

    gradient(kern_ref, got_ref, eig_ref, scale_ref, resid, head, 256, add)
    own_copy.wait()
    other_copy.wait()
    for copy in copies:
        copy.wait()


def take_step(core, kern, got, eig, scale, step, grad, weights, own, other):
    n, count = kern.shape
    c_dim = weights.shape[1]
    smem = pl.BlockSpec(memory_space=pltpu.SMEM)
    vmem = pl.BlockSpec(memory_space=pltpu.VMEM)
    hbm = pl.BlockSpec(memory_space=pltpu.HBM)
    return pl.pallas_call(
        step_kernel,
        in_specs=[smem] + [vmem] * 9,
        out_specs=[hbm] * 2,
        out_shape=(
            jax.ShapeDtypeStruct((2 * HALF, c_dim), F32),
            jax.ShapeDtypeStruct(weights.shape, F32),
        ),
        scratch_shapes=gradient_scratch(n, c_dim)
        + [
            pltpu.VMEM(weights.shape, F32),
            pltpu.SemaphoreType.DMA((4,)),
            pltpu.SemaphoreType.DMA((2,)),
        ],
        compiler_params=params(16),
        cost_estimate=pl.CostEstimate(
            flops=2 * n * count * c_dim, bytes_accessed=8 << 20, transcendentals=0
        ),
        name="take_step",
    )(core, kern, got, eig, scale, step, grad, weights, own, other)


def sq_norm(rows):
    return jnp.sum(rows.astype(F32) ** 2, axis=1) * scale_of(rows.shape[1])


def swap_cores(value):
    return lax.ppermute(value, "c", [(0, 1), (1, 0)])


def local(batch, targets, centers, weights, eigvec, eig_scale, step):
    core = lax.axis_index("c")
    half = core.reshape(1)
    n, d = BLOCKS * HALF, batch.shape[1]
    c_dim = weights.shape[1]

    first = lax.all_to_all(fan(half, batch), BLK, 0, 0, tiled=True).reshape(n, d)
    first, held, to_split = lax.optimization_barrier((first, centers, weights))
    second = swap_cores(first)
    cs = sq_norm(held)[None, :]
    weights3 = split_weights(to_split)
    sent, kern_first = terms(first, held, cs, weights3, eigvec)
    kept, kern_second = terms(second, held, cs, weights3, eigvec)
    coded = code(kept, swap_cores(sent)).astype(F16)

    got = lax.all_to_all(coded, PLANE, 0, 0, tiled=True)
    summed = decode(got.astype(F32)).reshape(RING_SIZE, RING_ROWS, LANES)
    pieces = ring_fan(lax.all_to_all(summed, "z", 0, 0, tiled=True))
    whole = lax.all_to_all(pieces, RING, 0, 0, tiled=True).reshape(2, WHOLE, LANES)

    own_pred, packed = pack(whole, targets, half)
    got_second = lax.all_to_all(packed, BLK, 0, 0, tiled=True)
    got_second, own_pred = lax.optimization_barrier((got_second, own_pred))
    got_first = swap_cores(got_second)
    other_pred = swap_cores(own_pred)
    scale = eig_scale[None, :]
    grad = half_gradient(kern_second, got_second, eigvec, scale, c_dim)
    return take_step(
        half,
        kern_first,
        got_first,
        eigvec,
        scale,
        step[None, :],
        grad,
        weights,
        own_pred,
        other_pred,
    )


def solution(mesh):
    fine = Mesh(mesh.devices.reshape(2, 4, 8, 2, 2), AXES)
    return jax.shard_map(
        local,
        mesh=fine,
        in_specs=(P(BLK, None), P(BLK, None), ALL, ALL, ALL, P(), P()),
        out_specs=(P(BLK, None), ALL),
        check_vma=False,
    )
```

```python
import math

import jax
import jax.numpy as jnp
from jax import lax
from jax.experimental import pallas as pl
from jax.experimental.pallas import tpu as pltpu
from jax.sharding import Mesh, PartitionSpec as P

AXES = ("xl", "y", "z", "xh", "c")
BLK = ("xl", "y")
PLANE = ("xl", "y", "xh")
ALL = P(AXES, None)
F32 = jnp.float32
BF16 = jnp.bfloat16
F16 = jnp.float16
NT = (((1,), (1,)), ((), ()))
NN = (((1,), (0,)), ((), ()))
TN = (((0,), (0,)), ((), ()))

HALF = 64
BLOCKS = 8
SUB = 32
SUBS = 16
LANES = 128
VALUE = 4 * SUB
MAIN = VALUE + SUB
PACKED = MAIN + 8
CODED = PACKED + 8
RING_SIZE = 8


def params(mib):
    return pltpu.CompilerParams(vmem_limit_bytes=mib << 20)


def split(value):
    high = value.astype(BF16)
    return high, (value - high.astype(F32)).astype(BF16)


def dot3(a, b, dims):
    a_hi, a_lo = split(a)
    b_hi, b_lo = split(b)

    def one(x, y):
        return lax.dot_general(x, y, dims, preferred_element_type=F32)

    return one(a_hi, b_hi) + one(a_hi, b_lo) + one(a_lo, b_hi)


def widen(eig):
    return jnp.concatenate([eig[:, :LANES]] + [eig[:, LANES:]] * 4, axis=1)


def lane_group(shape):
    return lax.broadcasted_iota(jnp.int32, shape, len(shape) - 1) // 32


def scale_of(features):
    return 4.0 / features * math.log2(math.e)


def fan_kernel(core_ref, hi_ref, blk_ref, rows_ref, out_ref):
    rows = rows_ref[...]
    for b in range(BLOCKS):
        out_ref[b] = rows


def fan(core, hi, blk, batch):
    d = batch.shape[1]
    return pl.pallas_call(
        fan_kernel,
        grid_spec=pltpu.PrefetchScalarGridSpec(
            num_scalar_prefetch=3,
            grid=(1,),
            in_specs=[pl.BlockSpec((HALF, d), lambda i, core, hi, blk: (1 - core[0], 0))],
            out_specs=pl.BlockSpec((BLOCKS, HALF, d), lambda i, core, hi, blk: (0, 0, 0)),
        ),
        out_shape=jax.ShapeDtypeStruct((BLOCKS, HALF, d), batch.dtype),
        compiler_params=params(8),
        name="fan",
    )(core, hi, blk, batch)


def weights_kernel(w_ref, out_ref):
    count = w_ref.shape[0]
    high, low = split(w_ref[...])
    out_ref[:count] = high
    out_ref[count : 2 * count] = low
    out_ref[2 * count :] = high


def split_weights(weights):
    count, c_dim = weights.shape
    return pl.pallas_call(
        weights_kernel,
        out_shape=jax.ShapeDtypeStruct((3 * count, c_dim), BF16),
        compiler_params=params(12),
        cost_estimate=pl.CostEstimate(flops=0, bytes_accessed=5 << 20, transcendentals=0),
        name="split_weights",
    )(weights)


def terms_kernel(rows_ref, cen_ref, cs_ref, w_ref, e_ref, out_ref, kern_ref, kern3):
    n, d = rows_ref.shape
    count = cen_ref.shape[0]
    tile = 512
    scale = scale_of(d)
    rows = rows_ref[...]
    wide = rows.astype(F32)
    rs = jnp.sum(wide * wide, axis=1, keepdims=True) * scale
    for at in range(0, count, tile):
        cols = slice(at, at + tile)
        cross = lax.dot_general(rows, cen_ref[cols, :], NT, preferred_element_type=F32)
        kern = jnp.exp2(cross * (2.0 * scale) - rs - cs_ref[:, cols])
        high, low = split(kern)
        kern3[:, at : at + tile] = high
        kern3[:, count + at : count + at + tile] = high
        kern_ref[:, cols] = high
        kern3[:, 2 * count + at : 2 * count + at + tile] = low
        if at == 0:
            coef = dot3(kern[:, :HALF], widen(e_ref[...]), NN)
            group = lane_group((8, LANES))
            for b in range(SUBS):
                block = coef[b * SUB : (b + 1) * SUB]
                out_ref[b, VALUE:MAIN, :] = block[:, :LANES]
                tail = block[:, LANES:]
                out_ref[b, MAIN:PACKED, :] = jnp.where(
                    group < 2,
                    jnp.where(group == 0, tail[0:8], tail[8:16]),
                    jnp.where(group == 2, tail[16:24], tail[24:32]),
                )
    value = lax.dot_general(kern3[...], w_ref[...], NN, preferred_element_type=F32)
    for b in range(SUBS):
        for j in range(4):
            out_ref[b, j * SUB : (j + 1) * SUB, :] = value[
                b * SUB : (b + 1) * SUB, j * LANES : (j + 1) * LANES
            ]


def terms(rows, centers, cs, weights3, eig):
    n, d = rows.shape
    count = centers.shape[0]
    c_dim = weights3.shape[1]
    return pl.pallas_call(
        terms_kernel,
        out_shape=(
            jax.ShapeDtypeStruct((SUBS, PACKED, LANES), F32),
            jax.ShapeDtypeStruct((n, count), BF16),
        ),
        scratch_shapes=[pltpu.VMEM((n, 3 * count), BF16)],
        compiler_params=params(24),
        cost_estimate=pl.CostEstimate(
            flops=20 * n * count * (d + 3 * c_dim), bytes_accessed=6 << 20, transcendentals=n * count
        ),
        name="terms",
    )(rows, centers, cs, weights3, eig)


def scaled(part):
    top = jnp.max(jnp.abs(part), axis=(0, 1), keepdims=True)
    power = jnp.ceil(jnp.log2(jnp.maximum(top, 1e-30)))
    return part * jnp.exp2(14.0 - power), power


def powers_tile(value_power, coef_power):
    upper = lax.broadcasted_iota(jnp.int32, (8, LANES), 0) < 4
    return jnp.where(upper, value_power, coef_power)


def unscale(ref, b):
    value = jnp.exp2(ref[b, PACKED : PACKED + 1, :] - 14.0)
    coef = jnp.exp2(ref[b, PACKED + 4 : PACKED + 5, :] - 14.0)
    return value, coef


def sum_blocks(ref):
    value = jnp.zeros((VALUE, LANES), F32)
    coef = jnp.zeros((PACKED - VALUE, LANES), F32)
    for b in range(ref.shape[0]):
        value_scale, coef_scale = unscale(ref, b)
        value += ref[b, :VALUE, :] * value_scale
        coef += ref[b, VALUE:PACKED, :] * coef_scale
    return value, coef


def code_kernel(a_ref, b_ref, out_ref):
    for b in range(a_ref.shape[0]):
        total = a_ref[b] + b_ref[b]
        value, value_power = scaled(total[:VALUE])
        coef, coef_power = scaled(total[VALUE:])
        out_ref[b, :VALUE, :] = value
        out_ref[b, VALUE:PACKED, :] = coef
        out_ref[b, PACKED:CODED, :] = powers_tile(value_power, coef_power)


def code(a, b):
    step = 8
    spec = pl.BlockSpec((step, PACKED, LANES), lambda i: (i, 0, 0))
    return pl.pallas_call(
        code_kernel,
        grid=(SUBS // step,),
        in_specs=[spec, spec],
        out_specs=pl.BlockSpec((step, CODED, LANES), lambda i: (i, 0, 0)),
        out_shape=jax.ShapeDtypeStruct((SUBS, CODED, LANES), F32),
        compiler_params=params(12),
        name="code",
    )(a, b)


def recode_kernel(x_ref, out_ref):
    value, coef = sum_blocks(x_ref)
    value, value_power = scaled(value)
    coef, coef_power = scaled(coef)
    out_ref[:VALUE, :] = value
    out_ref[VALUE:PACKED, :] = coef
    out_ref[PACKED:CODED, :] = powers_tile(value_power, coef_power)


def recode(x):
    return pl.pallas_call(
        recode_kernel,
        out_shape=jax.ShapeDtypeStruct((CODED, LANES), F32),
        compiler_params=params(12),
        name="recode",
    )(x)


def pack_kernel(core_ref, hi_ref, blk_ref, x_ref, targets_ref, out_ref):
    value, coef = sum_blocks(x_ref)
    row = pl.multiple_of(core_ref[0] * HALF + hi_ref[0] * SUB, SUB)
    resid = []
    for j in range(4):
        target = targets_ref[pl.ds(row, SUB), j * LANES : (j + 1) * LANES]
        resid.append(value[j * SUB : (j + 1) * SUB] - target)
    resid, resid_power = scaled(jnp.concatenate(resid, axis=0))
    value, value_power = scaled(value)
    coef, coef_power = scaled(coef)
    resid_tile = powers_tile(resid_power, coef_power)
    value_tile = powers_tile(value_power, coef_power)
    for b in range(SUBS):
        out_ref[b, :VALUE, :] = resid
        out_ref[b, VALUE:PACKED, :] = coef
        out_ref[b, PACKED:CODED, :] = resid_tile
    for h in range(2):
        b = blk_ref[0] * 2 + h
        out_ref[b, :VALUE, :] = value
        out_ref[b, PACKED:CODED, :] = value_tile


def pack(core, hi, blk, x, targets):
    smem = pl.BlockSpec(memory_space=pltpu.SMEM)
    vmem = pl.BlockSpec(memory_space=pltpu.VMEM)
    return pl.pallas_call(
        pack_kernel,
        in_specs=[smem] * 3 + [vmem] * 2,
        out_shape=jax.ShapeDtypeStruct((SUBS, CODED, LANES), F32),
        compiler_params=params(12),
        name="pack",
    )(core, hi, blk, x, targets)


def gradient(
    half, blk, kern_ref, got_ref, eig_ref, scale_ref, targets_ref, pred_ref, resid, head, tile, add
):
    count = kern_ref.shape[1]
    group = lane_group((8, LANES))
    coefs = []
    for b in range(SUBS):
        value_scale, coef_scale = unscale(got_ref, b)
        for j in range(4):
            resid[b * SUB : (b + 1) * SUB, j * LANES : (j + 1) * LANES] = (
                got_ref[b, j * SUB : (j + 1) * SUB, :] * value_scale
            ).astype(BF16)
        main = got_ref[b, VALUE:MAIN, :] * coef_scale
        tail = got_ref[b, MAIN:PACKED, :] * coef_scale
        tails = [jnp.where(group == t, tail, 0.0) for t in range(4)]
        coefs.append(jnp.concatenate([main, jnp.concatenate(tails, axis=0)], axis=1).astype(BF16))
    for h in range(2):
        b = blk * 2 + h
        value_scale, _ = unscale(got_ref, b)
        row = pl.multiple_of(half * HALF + h * SUB, SUB)
        for j in range(4):
            lanes = slice(j * LANES, (j + 1) * LANES)
            value = got_ref[b, j * SUB : (j + 1) * SUB, :] * value_scale
            pred_ref[h * SUB : (h + 1) * SUB, lanes] = value
            target = targets_ref[pl.ds(row, SUB), lanes]
            resid[pl.ds(pl.multiple_of(b * SUB, SUB), SUB), lanes] = (value - target).astype(BF16)
    coef = jnp.concatenate(coefs, axis=0)
    corr = jnp.zeros((coef.shape[0], HALF), F32)
    for part in split(widen(eig_ref[...] * scale_ref[...])):
        corr += lax.dot_general(coef, part, NT, preferred_element_type=F32)
    head[...] = kern_ref[:, :LANES]
    head[:, :HALF] = (kern_ref[:, :HALF].astype(F32) - corr).astype(BF16)
    for at in range(0, count, tile):
        if at == 0:
            kern = jnp.concatenate([head[...], kern_ref[:, LANES:tile]], axis=1)
        else:
            kern = kern_ref[:, at : at + tile]
        add(
            slice(at, at + tile),
            lax.dot_general(kern, resid[...], TN, preferred_element_type=F32),
        )


def gradient_scratch(n, c_dim):
    return [pltpu.VMEM((n, c_dim), BF16), pltpu.VMEM((n, LANES), BF16)]


def half_kernel(
    core_ref,
    blk_ref,
    kern_ref,
    got_ref,
    eig_ref,
    scale_ref,
    targets_ref,
    pred_ref,
    out_ref,
    resid,
    head,
):
    def add(rows, product):
        out_ref[rows, :] = product

    gradient(
        core_ref[0],
        blk_ref[0],
        kern_ref,
        got_ref,
        eig_ref,
        scale_ref,
        targets_ref,
        pred_ref,
        resid,
        head,
        512,
        add,
    )


def half_gradient(core, blk, kern, got, eig, scale, targets):
    n, count = kern.shape
    c_dim = targets.shape[1]
    smem = pl.BlockSpec(memory_space=pltpu.SMEM)
    vmem = pl.BlockSpec(memory_space=pltpu.VMEM)
    return pl.pallas_call(
        half_kernel,
        in_specs=[smem] * 2 + [vmem] * 5,
        out_shape=(
            jax.ShapeDtypeStruct((HALF, c_dim), F32),
            jax.ShapeDtypeStruct((count, c_dim), F32),
        ),
        scratch_shapes=gradient_scratch(n, c_dim),
        compiler_params=params(16),
        cost_estimate=pl.CostEstimate(
            flops=20 * n * count * c_dim, bytes_accessed=4 << 20, transcendentals=0
        ),
        name="half_gradient",
    )(core, blk, kern, got, eig, scale, targets)


def step_kernel(
    core_ref,
    blk_ref,
    kern_ref,
    got_ref,
    eig_ref,
    scale_ref,
    targets_ref,
    step_ref,
    grad_ref,
    w_ref,
    own_ref,
    pred_ref,
    out_ref,
    resid,
    head,
    other,
    new,
    sem,
    pred_sem,
):
    core = core_ref[0]
    own_copy = pltpu.make_async_copy(
        own_ref, pred_ref.at[pl.ds(pl.multiple_of(core * HALF, HALF), HALF)], pred_sem.at[0]
    )
    own_copy.start()
    step = step_ref[...]
    copies = []

    def add(rows, product):
        new[rows, :] = w_ref[rows, :] - step * (grad_ref[rows, :] + product)
        k = len(copies)
        copies.append(pltpu.make_async_copy(new.at[rows], out_ref.at[rows], sem.at[k]))
        copies[k].start()

    gradient(
        1 - core,
        blk_ref[0],
        kern_ref,
        got_ref,
        eig_ref,
        scale_ref,
        targets_ref,
        other,
        resid,
        head,
        256,
        add,
    )
    other_copy = pltpu.make_async_copy(
        other, pred_ref.at[pl.ds(pl.multiple_of((1 - core) * HALF, HALF), HALF)], pred_sem.at[1]
    )
    other_copy.start()
    own_copy.wait()
    for copy in copies:
        copy.wait()
    other_copy.wait()


def take_step(core, blk, kern, got, eig, scale, targets, step, grad, weights, own):
    n, count = kern.shape
    c_dim = weights.shape[1]
    smem = pl.BlockSpec(memory_space=pltpu.SMEM)
    vmem = pl.BlockSpec(memory_space=pltpu.VMEM)
    hbm = pl.BlockSpec(memory_space=pltpu.HBM)
    return pl.pallas_call(
        step_kernel,
        in_specs=[smem] * 2 + [vmem] * 9,
        out_specs=[hbm] * 2,
        out_shape=(
            jax.ShapeDtypeStruct(targets.shape, F32),
            jax.ShapeDtypeStruct(weights.shape, F32),
        ),
        scratch_shapes=gradient_scratch(n, c_dim)
        + [
            pltpu.VMEM((HALF, c_dim), F32),
            pltpu.VMEM(weights.shape, F32),
            pltpu.SemaphoreType.DMA((4,)),
            pltpu.SemaphoreType.DMA((2,)),
        ],
        compiler_params=params(16),
        cost_estimate=pl.CostEstimate(
            flops=2 * n * count * c_dim, bytes_accessed=8 << 20, transcendentals=0
        ),
        name="take_step",
    )(core, blk, kern, got, eig, scale, targets, step, grad, weights, own)


def sq_norm(rows):
    return jnp.sum(rows.astype(F32) ** 2, axis=1) * scale_of(rows.shape[1])


def swap_cores(value):
    return lax.ppermute(value, "c", [(0, 1), (1, 0)])


def local(batch, targets, centers, weights, eigvec, eig_scale, step):
    core = lax.axis_index("c").reshape(1)
    hi = lax.axis_index("xh").reshape(1)
    blk = lax.axis_index(BLK).reshape(1)
    n, d = BLOCKS * HALF, batch.shape[1]

    first = lax.all_to_all(fan(core, hi, blk, batch), BLK, 0, 0, tiled=True).reshape(n, d)
    first, held, to_split = lax.optimization_barrier((first, centers, weights))
    second = swap_cores(first)
    cs = sq_norm(held)[None, :]
    weights3 = split_weights(to_split)
    sent, kern_first = terms(first, held, cs, weights3, eigvec)
    kept, kern_second = terms(second, held, cs, weights3, eigvec)
    coded = code(kept, swap_cores(sent)).astype(F16)

    got = lax.all_to_all(coded, PLANE, 0, 0, tiled=True).astype(F32)
    partial = recode(got).astype(F16)
    partial = jnp.broadcast_to(partial[None], (RING_SIZE,) + partial.shape)
    ring = lax.all_to_all(partial, "z", 0, 0, tiled=True).astype(F32)

    packed = pack(core, hi, blk, ring, targets).astype(F16)
    got_second = lax.all_to_all(packed, PLANE, 0, 0, tiled=True)
    got_first = swap_cores(got_second)
    scale = eig_scale[None, :]
    own, grad = half_gradient(
        core, blk, kern_second, got_second.astype(F32), eigvec, scale, targets
    )
    return take_step(
        core,
        blk,
        kern_first,
        got_first.astype(F32),
        eigvec,
        scale,
        targets,
        step[None, :],
        grad,
        weights,
        own,
    )


def solution(mesh):
    fine = Mesh(mesh.devices.reshape(2, 4, 8, 2, 2), AXES)
    return jax.shard_map(
        local,
        mesh=fine,
        in_specs=(P(BLK, None), P(BLK, None), ALL, ALL, ALL, P(), P()),
        out_specs=(P(BLK, None), ALL),
        check_vma=False,
    )
```

```python
import math

import jax
import jax.numpy as jnp
from jax import lax
from jax.experimental import pallas as pl
from jax.experimental.pallas import tpu as pltpu
from jax.sharding import Mesh, PartitionSpec as P

AXES = ("xl", "y", "zh", "zl", "xh", "c")
BLK = ("xl", "y")
SUB_AXES = ("xh", "zl")
NEAR = BLK + SUB_AXES
FAR = "zh"
ALL = P(AXES, None)
F32 = jnp.float32
BF16 = jnp.bfloat16
F16 = jnp.float16
NT = (((1,), (1,)), ((), ()))
NN = (((1,), (0,)), ((), ()))
TN = (((0,), (0,)), ((), ()))

HALF = 64
BLOCKS = 8
SUB = 16
SUBS = 32
PER_BLOCK = HALF // SUB
LANES = 128
VALUE = 4 * SUB
MAIN = VALUE + SUB
CODED = MAIN + 8
FAR_SIZE = 4


def params(mib):
    return pltpu.CompilerParams(vmem_limit_bytes=mib << 20)


def split(value):
    high = value.astype(BF16)
    return high, (value - high.astype(F32)).astype(BF16)


def dot3(a, b, dims):
    a_hi, a_lo = split(a)
    b_hi, b_lo = split(b)

    def one(x, y):
        return lax.dot_general(x, y, dims, preferred_element_type=F32)

    return one(a_hi, b_hi) + one(a_hi, b_lo) + one(a_lo, b_hi)


def widen(eig):
    return jnp.concatenate([eig[:, :LANES]] + [eig[:, LANES:]] * 4, axis=1)


def lane_group(shape):
    return lax.broadcasted_iota(jnp.int32, shape, len(shape) - 1) // 32


def scale_of(features):
    return 4.0 / features * math.log2(math.e)


def fan_kernel(core_ref, sub_ref, blk_ref, rows_ref, out_ref):
    rows = rows_ref[...]
    for b in range(BLOCKS):
        out_ref[b] = rows


def fan(core, sub, blk, batch):
    d = batch.shape[1]
    return pl.pallas_call(
        fan_kernel,
        grid_spec=pltpu.PrefetchScalarGridSpec(
            num_scalar_prefetch=3,
            grid=(1,),
            in_specs=[pl.BlockSpec((HALF, d), lambda i, core, sub, blk: (1 - core[0], 0))],
            out_specs=pl.BlockSpec((BLOCKS, HALF, d), lambda i, core, sub, blk: (0, 0, 0)),
        ),
        out_shape=jax.ShapeDtypeStruct((BLOCKS, HALF, d), batch.dtype),
        compiler_params=params(8),
        name="fan",
    )(core, sub, blk, batch)


def weights_kernel(w_ref, e_ref, out_ref, e_out):
    count = w_ref.shape[0]
    e_out[...] = widen(e_ref[...])
    high, low = split(w_ref[...])
    out_ref[:count] = high
    out_ref[count : 2 * count] = low
    out_ref[2 * count :] = high


def split_weights(weights, eig):
    count, c_dim = weights.shape
    return pl.pallas_call(
        weights_kernel,
        out_shape=(
            jax.ShapeDtypeStruct((3 * count, c_dim), BF16),
            jax.ShapeDtypeStruct((HALF, 2 * LANES), F32),
        ),
        compiler_params=params(12),
        cost_estimate=pl.CostEstimate(flops=0, bytes_accessed=5 << 20, transcendentals=0),
        name="split_weights",
    )(weights, eig)


def terms_kernel(rows_ref, cen_ref, cs_ref, w_ref, e_ref, out_ref, kern_ref, kern3):
    n, d = rows_ref.shape
    count = cen_ref.shape[0]
    tile = 512
    scale = scale_of(d)
    rows = rows_ref[...]
    wide = rows.astype(F32)
    rs = jnp.sum(wide * wide, axis=1, keepdims=True) * scale
    for at in range(0, count, tile):
        cols = slice(at, at + tile)
        cross = lax.dot_general(rows, cen_ref[cols, :], NT, preferred_element_type=F32)
        kern = jnp.exp2(cross * (2.0 * scale) - rs - cs_ref[:, cols])
        high, low = split(kern)
        kern3[:, at : at + tile] = high
        kern3[:, count + at : count + at + tile] = high
        kern_ref[:, cols] = high
        kern3[:, 2 * count + at : 2 * count + at + tile] = low
        if at == 0:
            coef = dot3(kern[:, :HALF], e_ref[...], NN)
            group = lane_group((8, LANES))
            for b in range(SUBS):
                block = coef[b * SUB : (b + 1) * SUB]
                out_ref[b, VALUE:MAIN, :] = block[:, :LANES]
                tail = block[:, LANES:]
                out_ref[b, MAIN:CODED, :] = jnp.where(
                    group == 0, tail[:8], jnp.where(group == 1, tail[8:], 0.0)
                )
    value = lax.dot_general(kern3[...], w_ref[...], NN, preferred_element_type=F32)
    for b in range(SUBS):
        for j in range(4):
            out_ref[b, j * SUB : (j + 1) * SUB, :] = value[
                b * SUB : (b + 1) * SUB, j * LANES : (j + 1) * LANES
            ]


def terms(rows, centers, cs, weights3, eig):
    n, d = rows.shape
    count = centers.shape[0]
    c_dim = weights3.shape[1]
    return pl.pallas_call(
        terms_kernel,
        out_shape=(
            jax.ShapeDtypeStruct((SUBS, CODED, LANES), F32),
            jax.ShapeDtypeStruct((n, count), BF16),
        ),
        scratch_shapes=[pltpu.VMEM((n, 3 * count), BF16)],
        compiler_params=params(24),
        cost_estimate=pl.CostEstimate(
            flops=20 * n * count * (d + 3 * c_dim), bytes_accessed=6 << 20, transcendentals=n * count
        ),
        name="terms",
    )(rows, centers, cs, weights3, eig)


def scaled(part):
    top = jnp.max(jnp.abs(part), axis=(0, 1), keepdims=True)
    power = jnp.ceil(jnp.log2(jnp.maximum(top, 1e-30)))
    return part * jnp.exp2(14.0 - power), power


def with_powers(coef, value_power, coef_power):
    group = lane_group((8, LANES))
    powers = jnp.where(group == 2, value_power, coef_power)
    tile = jnp.where(group < 2, coef[SUB:], powers)
    return coef[:SUB], tile


def unscale(ref, b):
    value = jnp.exp2(ref[b, MAIN : MAIN + 1, 64:65] - 14.0)
    coef = jnp.exp2(ref[b, MAIN : MAIN + 1, 96:97] - 14.0)
    return value, coef


def sum_blocks(ref):
    value = jnp.zeros((VALUE, LANES), F32)
    main = jnp.zeros((SUB, LANES), F32)
    tile = jnp.zeros((8, LANES), F32)
    for b in range(ref.shape[0]):
        value_scale, coef_scale = unscale(ref, b)
        value += ref[b, :VALUE, :] * value_scale
        main += ref[b, VALUE:MAIN, :] * coef_scale
        tile += ref[b, MAIN:CODED, :] * coef_scale
    tile = jnp.where(lane_group((8, LANES)) < 2, tile, 0.0)
    return value, jnp.concatenate([main, tile], axis=0)


def code_kernel(a_ref, b_ref, out_ref):
    for b in range(SUBS):
        total = a_ref[b] + b_ref[b]
        value, value_power = scaled(total[:VALUE])
        coef, coef_power = scaled(total[VALUE:])
        main, tile = with_powers(coef, value_power, coef_power)
        out_ref[b, :VALUE, :] = value
        out_ref[b, VALUE:MAIN, :] = main
        out_ref[b, MAIN:CODED, :] = tile


def code(a, b):
    return pl.pallas_call(
        code_kernel,
        out_shape=jax.ShapeDtypeStruct((SUBS, CODED, LANES), F32),
        compiler_params=params(12),
        name="code",
    )(a, b)


def recode_kernel(x_ref, out_ref):
    value, coef = sum_blocks(x_ref)
    value, value_power = scaled(value)
    coef, coef_power = scaled(coef)
    main, tile = with_powers(coef, value_power, coef_power)
    out_ref[:VALUE, :] = value
    out_ref[VALUE:MAIN, :] = main
    out_ref[MAIN:CODED, :] = tile


def recode(x):
    return pl.pallas_call(
        recode_kernel,
        out_shape=jax.ShapeDtypeStruct((CODED, LANES), F32),
        compiler_params=params(12),
        name="recode",
    )(x)


def pack_kernel(core_ref, sub_ref, blk_ref, x_ref, targets_ref, out_ref):
    value, coef = sum_blocks(x_ref)
    row = pl.multiple_of(core_ref[0] * HALF + sub_ref[0] * SUB, SUB)
    resid = []
    for j in range(4):
        target = targets_ref[pl.ds(row, SUB), j * LANES : (j + 1) * LANES]
        resid.append(value[j * SUB : (j + 1) * SUB] - target)
    resid, resid_power = scaled(jnp.concatenate(resid, axis=0))
    value, value_power = scaled(value)
    coef, coef_power = scaled(coef)
    main, tile = with_powers(coef, resid_power, coef_power)
    for b in range(SUBS):
        out_ref[b, :VALUE, :] = resid
        out_ref[b, VALUE:MAIN, :] = main
        out_ref[b, MAIN:CODED, :] = tile
    _, tile = with_powers(coef, value_power, coef_power)
    for h in range(PER_BLOCK):
        b = blk_ref[0] * PER_BLOCK + h
        out_ref[b, :VALUE, :] = value
        out_ref[b, MAIN:CODED, :] = tile


def pack(core, sub, blk, x, targets):
    smem = pl.BlockSpec(memory_space=pltpu.SMEM)
    vmem = pl.BlockSpec(memory_space=pltpu.VMEM)
    return pl.pallas_call(
        pack_kernel,
        in_specs=[smem] * 3 + [vmem] * 2,
        out_shape=jax.ShapeDtypeStruct((SUBS, CODED, LANES), F32),
        compiler_params=params(12),
        name="pack",
    )(core, sub, blk, x, targets)


def gradient(
    half, blk, kern_ref, got_ref, eig_ref, scale_ref, targets_ref, pred_ref, resid, head, tile, add
):
    count = kern_ref.shape[1]
    group = lane_group((8, LANES))
    coefs = []
    for b in range(SUBS):
        value_scale, coef_scale = unscale(got_ref, b)
        for j in range(4):
            resid[b * SUB : (b + 1) * SUB, j * LANES : (j + 1) * LANES] = (
                got_ref[b, j * SUB : (j + 1) * SUB, :] * value_scale
            ).astype(BF16)
        main = got_ref[b, VALUE:MAIN, :] * coef_scale
        tile_rows = got_ref[b, MAIN:CODED, :] * coef_scale
        tails = [jnp.where(group == t, tile_rows, 0.0) for t in range(2)]
        coefs.append(jnp.concatenate([main, jnp.concatenate(tails, axis=0)], axis=1).astype(BF16))
    for h in range(PER_BLOCK):
        b = blk * PER_BLOCK + h
        value_scale, _ = unscale(got_ref, b)
        row = pl.multiple_of(half * HALF + h * SUB, SUB)
        for j in range(4):
            lanes = slice(j * LANES, (j + 1) * LANES)
            value = got_ref[b, j * SUB : (j + 1) * SUB, :] * value_scale
            pred_ref[h * SUB : (h + 1) * SUB, lanes] = value
            target = targets_ref[pl.ds(row, SUB), lanes]
            resid[pl.ds(pl.multiple_of(b * SUB, SUB), SUB), lanes] = (value - target).astype(BF16)
    coef = jnp.concatenate(coefs, axis=0)
    corr = jnp.zeros((coef.shape[0], HALF), F32)
    for part in split(eig_ref[...] * widen(scale_ref[:, : LANES + 32])):
        corr += lax.dot_general(coef, part, NT, preferred_element_type=F32)
    head[...] = kern_ref[:, :LANES]
    head[:, :HALF] = (kern_ref[:, :HALF].astype(F32) - corr).astype(BF16)
    for at in [*range(tile, count, tile), 0]:
        if at == 0:
            kern = jnp.concatenate([head[...], kern_ref[:, LANES:tile]], axis=1)
        else:
            kern = kern_ref[:, at : at + tile]
        add(
            slice(at, at + tile),
            lax.dot_general(kern, resid[...], TN, preferred_element_type=F32),
        )


def gradient_scratch(n, c_dim):
    return [pltpu.VMEM((n, c_dim), BF16), pltpu.VMEM((n, LANES), BF16)]


def half_kernel(
    core_ref,
    blk_ref,
    kern_ref,
    got_ref,
    eig_ref,
    scale_ref,
    targets_ref,
    w_ref,
    pred_ref,
    out_ref,
    resid,
    head,
):
    step = scale_ref[:, LANES + 32 :]

    def add(rows, product):
        out_ref[rows, :] = w_ref[rows, :] - step * product

    gradient(
        core_ref[0],
        blk_ref[0],
        kern_ref,
        got_ref,
        eig_ref,
        scale_ref,
        targets_ref,
        pred_ref,
        resid,
        head,
        512,
        add,
    )


def half_step(core, blk, kern, got, eig, scale, targets, weights):
    n, count = kern.shape
    c_dim = targets.shape[1]
    smem = pl.BlockSpec(memory_space=pltpu.SMEM)
    vmem = pl.BlockSpec(memory_space=pltpu.VMEM)
    return pl.pallas_call(
        half_kernel,
        in_specs=[smem] * 2 + [vmem] * 6,
        out_shape=(
            jax.ShapeDtypeStruct((HALF, c_dim), F32),
            jax.ShapeDtypeStruct((count, c_dim), F32),
        ),
        scratch_shapes=gradient_scratch(n, c_dim),
        compiler_params=params(16),
        cost_estimate=pl.CostEstimate(
            flops=20 * n * count * c_dim, bytes_accessed=4 << 20, transcendentals=0
        ),
        name="half_step",
    )(core, blk, kern, got, eig, scale, targets, weights)


def step_kernel(
    core_ref,
    blk_ref,
    kern_ref,
    got_ref,
    eig_ref,
    scale_ref,
    targets_ref,
    base_ref,
    own_ref,
    pred_ref,
    out_ref,
    resid,
    head,
    other,
    new,
    sem,
    pred_sem,
):
    core = core_ref[0]
    own_copy = pltpu.make_async_copy(
        own_ref, pred_ref.at[pl.ds(pl.multiple_of(core * HALF, HALF), HALF)], pred_sem.at[0]
    )
    own_copy.start()
    step = scale_ref[:, LANES + 32 :]
    copies = []

    def add(rows, product):
        new[rows, :] = base_ref[rows, :] - step * product
        k = len(copies)
        copies.append(pltpu.make_async_copy(new.at[rows], out_ref.at[rows], sem.at[k]))
        copies[k].start()

    gradient(
        1 - core,
        blk_ref[0],
        kern_ref,
        got_ref,
        eig_ref,
        scale_ref,
        targets_ref,
        other,
        resid,
        head,
        256,
        add,
    )
    other_copy = pltpu.make_async_copy(
        other, pred_ref.at[pl.ds(pl.multiple_of((1 - core) * HALF, HALF), HALF)], pred_sem.at[1]
    )
    other_copy.start()
    own_copy.wait()
    for copy in copies:
        copy.wait()
    other_copy.wait()


def take_step(core, blk, kern, got, eig, scale, targets, base, own):
    n, count = kern.shape
    c_dim = base.shape[1]
    smem = pl.BlockSpec(memory_space=pltpu.SMEM)
    vmem = pl.BlockSpec(memory_space=pltpu.VMEM)
    hbm = pl.BlockSpec(memory_space=pltpu.HBM)
    return pl.pallas_call(
        step_kernel,
        in_specs=[smem] * 2 + [vmem] * 7,
        out_specs=[hbm] * 2,
        out_shape=(
            jax.ShapeDtypeStruct(targets.shape, F32),
            jax.ShapeDtypeStruct(base.shape, F32),
        ),
        scratch_shapes=gradient_scratch(n, c_dim)
        + [
            pltpu.VMEM((HALF, c_dim), F32),
            pltpu.VMEM(base.shape, F32),
            pltpu.SemaphoreType.DMA((4,)),
            pltpu.SemaphoreType.DMA((2,)),
        ],
        compiler_params=params(16),
        cost_estimate=pl.CostEstimate(
            flops=2 * n * count * c_dim, bytes_accessed=8 << 20, transcendentals=0
        ),
        name="take_step",
    )(core, blk, kern, got, eig, scale, targets, base, own)


def sq_norm(rows):
    return jnp.sum(rows.astype(F32) ** 2, axis=1) * scale_of(rows.shape[1])


def swap_cores(value):
    return lax.ppermute(value, "c", [(0, 1), (1, 0)])


def local(batch, targets, centers, weights, eigvec, eig_scale, step):
    core = lax.axis_index("c").reshape(1)
    sub = lax.axis_index(SUB_AXES).reshape(1)
    blk = lax.axis_index(BLK).reshape(1)
    n, d = BLOCKS * HALF, batch.shape[1]

    first = lax.all_to_all(fan(core, sub, blk, batch), BLK, 0, 0, tiled=True).reshape(n, d)
    first, held, to_split = lax.optimization_barrier((first, centers, weights))
    second = swap_cores(first)
    cs = sq_norm(held)[None, :]
    weights3, eig = split_weights(to_split, eigvec)
    sent, kern_first = terms(first, held, cs, weights3, eig)
    kept, kern_second = terms(second, held, cs, weights3, eig)
    coded = code(kept, swap_cores(sent)).astype(F16)

    got = lax.all_to_all(coded, NEAR, 0, 0, tiled=True).astype(F32)
    partial = recode(got).astype(F16)
    partial = jnp.broadcast_to(partial[None], (FAR_SIZE,) + partial.shape)
    far = lax.all_to_all(partial, FAR, 0, 0, tiled=True).astype(F32)

    packed = pack(core, sub, blk, far, targets).astype(F16)
    got_second = lax.all_to_all(packed, NEAR, 0, 0, tiled=True)
    got_first = swap_cores(got_second)
    scale = jnp.concatenate([eig_scale, step])[None, :]
    own, base = half_step(
        core, blk, kern_second, got_second.astype(F32), eig, scale, targets, weights
    )
    return take_step(
        core, blk, kern_first, got_first.astype(F32), eig, scale, targets, base, own
    )


def solution(mesh):
    fine = Mesh(mesh.devices.reshape(2, 4, 4, 2, 2, 2), AXES)
    return jax.shard_map(
        local,
        mesh=fine,
        in_specs=(P(BLK, None), P(BLK, None), ALL, ALL, ALL, P(), P()),
        out_specs=(P(BLK, None), ALL),
        check_vma=False,
    )
```

```python
import math

import jax
import jax.numpy as jnp
from jax import lax
from jax.experimental import pallas as pl
from jax.experimental.pallas import tpu as pltpu
from jax.sharding import Mesh, PartitionSpec as P

AXES = ("xl", "y", "zh", "zl", "xh", "c")
BLK = ("xl", "y")
SUB_AXES = ("xh", "zl")
NEAR = BLK + SUB_AXES
FAR = "zh"
ALL = P(AXES, None)
F32 = jnp.float32
BF16 = jnp.bfloat16
F16 = jnp.float16
NT = (((1,), (1,)), ((), ()))
NN = (((1,), (0,)), ((), ()))
TN = (((0,), (0,)), ((), ()))

HALF = 64
BLOCKS = 8
SUB = 16
SUBS = 32
PER_BLOCK = HALF // SUB
LANES = 128
VALUE = 4 * SUB
MAIN = VALUE + SUB
CODED = MAIN + 8
FAR_SIZE = 4


def params(mib):
    return pltpu.CompilerParams(vmem_limit_bytes=mib << 20)


def split(value):
    high = value.astype(BF16)
    return high, (value - high.astype(F32)).astype(BF16)


def dot3(a, b, dims):
    a_hi, a_lo = split(a)
    b_hi, b_lo = split(b)

    def one(x, y):
        return lax.dot_general(x, y, dims, preferred_element_type=F32)

    return one(a_hi, b_hi) + one(a_hi, b_lo) + one(a_lo, b_hi)


def widen(eig):
    return jnp.concatenate([eig[:, :LANES]] + [eig[:, LANES:]] * 4, axis=1)


def lane_group(shape):
    return lax.broadcasted_iota(jnp.int32, shape, len(shape) - 1) // 32


def scale_of(features):
    return 4.0 / features * math.log2(math.e)


def fan_kernel(core_ref, sub_ref, blk_ref, rows_ref, out_ref):
    rows = rows_ref[...]
    for b in range(BLOCKS):
        out_ref[b] = rows


def fan(core, sub, blk, batch):
    d = batch.shape[1]
    return pl.pallas_call(
        fan_kernel,
        grid_spec=pltpu.PrefetchScalarGridSpec(
            num_scalar_prefetch=3,
            grid=(1,),
            in_specs=[pl.BlockSpec((HALF, d), lambda i, core, sub, blk: (1 - core[0], 0))],
            out_specs=pl.BlockSpec((BLOCKS, HALF, d), lambda i, core, sub, blk: (0, 0, 0)),
        ),
        out_shape=jax.ShapeDtypeStruct((BLOCKS, HALF, d), batch.dtype),
        compiler_params=params(8),
        name="fan",
    )(core, sub, blk, batch)


def terms_body(rows_ref, cen_ref, cs_ref, eig, weights3, out_ref, kern_ref, kern3):
    n, d = rows_ref.shape
    count = cen_ref.shape[0]
    tile = 512
    scale = scale_of(d)
    rows = rows_ref[...]
    wide = rows.astype(F32)
    rs = jnp.sum(wide * wide, axis=1, keepdims=True) * scale
    for at in range(0, count, tile):
        cols = slice(at, at + tile)
        cross = lax.dot_general(rows, cen_ref[cols, :], NT, preferred_element_type=F32)
        kern = jnp.exp2(cross * (2.0 * scale) - rs - cs_ref[:, cols])
        high, low = split(kern)
        kern3[:, at : at + tile] = high
        kern3[:, count + at : count + at + tile] = high
        kern_ref[:, cols] = high
        kern3[:, 2 * count + at : 2 * count + at + tile] = low
        if at == 0:
            coef = dot3(kern[:, :HALF], eig, NN)
            group = lane_group((8, LANES))
            for b in range(SUBS):
                block = coef[b * SUB : (b + 1) * SUB]
                out_ref[b, VALUE:MAIN, :] = block[:, :LANES]
                tail = block[:, LANES:]
                out_ref[b, MAIN:CODED, :] = jnp.where(
                    group == 0, tail[:8], jnp.where(group == 1, tail[8:], 0.0)
                )
    value = lax.dot_general(kern3[...], weights3(), NN, preferred_element_type=F32)
    for b in range(SUBS):
        for j in range(4):
            out_ref[b, j * SUB : (j + 1) * SUB, :] = value[
                b * SUB : (b + 1) * SUB, j * LANES : (j + 1) * LANES
            ]


def first_kernel(rows_ref, cen_ref, cs_ref, w_ref, e_ref, out_ref, kern_ref, w3_ref, e_out, kern3):
    eig = widen(e_ref[...])
    e_out[...] = eig

    def weights3():
        count = w_ref.shape[0]
        high, low = split(w_ref[...])
        w3_ref[:count] = high
        w3_ref[count : 2 * count] = low
        w3_ref[2 * count :] = high
        return w3_ref[...]

    terms_body(rows_ref, cen_ref, cs_ref, eig, weights3, out_ref, kern_ref, kern3)


def second_kernel(rows_ref, cen_ref, cs_ref, w3_ref, e_ref, out_ref, kern_ref, kern3):
    terms_body(
        rows_ref, cen_ref, cs_ref, e_ref[...], lambda: w3_ref[...], out_ref, kern_ref, kern3
    )


def terms(kernel, rows, centers, cs, weights, eig, extra=()):
    n, d = rows.shape
    count = centers.shape[0]
    c_dim = weights.shape[1]
    return pl.pallas_call(
        kernel,
        out_shape=(
            jax.ShapeDtypeStruct((SUBS, CODED, LANES), F32),
            jax.ShapeDtypeStruct((n, count), BF16),
        )
        + extra,
        scratch_shapes=[pltpu.VMEM((n, 3 * count), BF16)],
        compiler_params=params(24),
        cost_estimate=pl.CostEstimate(
            flops=20 * n * count * (d + 3 * c_dim), bytes_accessed=6 << 20, transcendentals=n * count
        ),
        name="terms",
    )(rows, centers, cs, weights, eig)


def scaled(part):
    top = jnp.max(jnp.abs(part), axis=(0, 1), keepdims=True)
    power = jnp.ceil(jnp.log2(jnp.maximum(top, 1e-30)))
    return part * jnp.exp2(14.0 - power), power


def with_powers(coef, value_power, coef_power):
    group = lane_group((8, LANES))
    powers = jnp.where(group == 2, value_power, coef_power)
    tile = jnp.where(group < 2, coef[SUB:], powers)
    return coef[:SUB], tile


def unscale(ref, b):
    value = jnp.exp2(ref[b, MAIN : MAIN + 1, 64:65] - 14.0)
    coef = jnp.exp2(ref[b, MAIN : MAIN + 1, 96:97] - 14.0)
    return value, coef


def sum_blocks(ref):
    value = jnp.zeros((VALUE, LANES), F32)
    main = jnp.zeros((SUB, LANES), F32)
    tile = jnp.zeros((8, LANES), F32)
    for b in range(ref.shape[0]):
        value_scale, coef_scale = unscale(ref, b)
        value += ref[b, :VALUE, :] * value_scale
        main += ref[b, VALUE:MAIN, :] * coef_scale
        tile += ref[b, MAIN:CODED, :] * coef_scale
    tile = jnp.where(lane_group((8, LANES)) < 2, tile, 0.0)
    return value, jnp.concatenate([main, tile], axis=0)


def code_kernel(a_ref, b_ref, out_ref):
    for b in range(SUBS):
        total = a_ref[b] + b_ref[b]
        value, value_power = scaled(total[:VALUE])
        coef, coef_power = scaled(total[VALUE:])
        main, tile = with_powers(coef, value_power, coef_power)
        out_ref[b, :VALUE, :] = value
        out_ref[b, VALUE:MAIN, :] = main
        out_ref[b, MAIN:CODED, :] = tile


def code(a, b):
    return pl.pallas_call(
        code_kernel,
        out_shape=jax.ShapeDtypeStruct((SUBS, CODED, LANES), F32),
        compiler_params=params(12),
        name="code",
    )(a, b)


def recode_kernel(x_ref, out_ref):
    value, coef = sum_blocks(x_ref)
    value, value_power = scaled(value)
    coef, coef_power = scaled(coef)
    main, tile = with_powers(coef, value_power, coef_power)
    out_ref[:VALUE, :] = value
    out_ref[VALUE:MAIN, :] = main
    out_ref[MAIN:CODED, :] = tile


def recode(x):
    return pl.pallas_call(
        recode_kernel,
        out_shape=jax.ShapeDtypeStruct((CODED, LANES), F32),
        compiler_params=params(12),
        name="recode",
    )(x)


def pack_kernel(core_ref, sub_ref, blk_ref, x_ref, targets_ref, out_ref):
    value, coef = sum_blocks(x_ref)
    row = pl.multiple_of(core_ref[0] * HALF + sub_ref[0] * SUB, SUB)
    resid = []
    for j in range(4):
        target = targets_ref[pl.ds(row, SUB), j * LANES : (j + 1) * LANES]
        resid.append(value[j * SUB : (j + 1) * SUB] - target)
    resid, resid_power = scaled(jnp.concatenate(resid, axis=0))
    value, value_power = scaled(value)
    coef, coef_power = scaled(coef)
    main, tile = with_powers(coef, resid_power, coef_power)
    for b in range(SUBS):
        out_ref[b, :VALUE, :] = resid
        out_ref[b, VALUE:MAIN, :] = main
        out_ref[b, MAIN:CODED, :] = tile
    _, tile = with_powers(coef, value_power, coef_power)
    for h in range(PER_BLOCK):
        b = blk_ref[0] * PER_BLOCK + h
        out_ref[b, :VALUE, :] = value
        out_ref[b, MAIN:CODED, :] = tile


def pack(core, sub, blk, x, targets):
    smem = pl.BlockSpec(memory_space=pltpu.SMEM)
    vmem = pl.BlockSpec(memory_space=pltpu.VMEM)
    return pl.pallas_call(
        pack_kernel,
        in_specs=[smem] * 3 + [vmem] * 2,
        out_shape=jax.ShapeDtypeStruct((SUBS, CODED, LANES), F32),
        compiler_params=params(12),
        name="pack",
    )(core, sub, blk, x, targets)


def gradient(
    half, blk, kern_ref, got_ref, eig_ref, scale_ref, targets_ref, pred_ref, resid, head, tile, add
):
    count = kern_ref.shape[1]
    group = lane_group((8, LANES))
    coefs = []
    for b in range(SUBS):
        value_scale, coef_scale = unscale(got_ref, b)
        for j in range(4):
            resid[b * SUB : (b + 1) * SUB, j * LANES : (j + 1) * LANES] = (
                got_ref[b, j * SUB : (j + 1) * SUB, :] * value_scale
            ).astype(BF16)
        main = got_ref[b, VALUE:MAIN, :] * coef_scale
        tile_rows = got_ref[b, MAIN:CODED, :] * coef_scale
        tails = [jnp.where(group == t, tile_rows, 0.0) for t in range(2)]
        coefs.append(jnp.concatenate([main, jnp.concatenate(tails, axis=0)], axis=1).astype(BF16))
    for h in range(PER_BLOCK):
        b = blk * PER_BLOCK + h
        value_scale, _ = unscale(got_ref, b)
        row = pl.multiple_of(half * HALF + h * SUB, SUB)
        for j in range(4):
            lanes = slice(j * LANES, (j + 1) * LANES)
            value = got_ref[b, j * SUB : (j + 1) * SUB, :] * value_scale
            pred_ref[h * SUB : (h + 1) * SUB, lanes] = value
            target = targets_ref[pl.ds(row, SUB), lanes]
            resid[pl.ds(pl.multiple_of(b * SUB, SUB), SUB), lanes] = (value - target).astype(BF16)
    coef = jnp.concatenate(coefs, axis=0)
    corr = jnp.zeros((coef.shape[0], HALF), F32)
    for part in split(eig_ref[...] * widen(scale_ref[:, : LANES + 32])):
        corr += lax.dot_general(coef, part, NT, preferred_element_type=F32)
    head[...] = kern_ref[:, :LANES]
    head[:, :HALF] = (kern_ref[:, :HALF].astype(F32) - corr).astype(BF16)
    for at in [*range(tile, count, tile), 0]:
        if at == 0:
            kern = jnp.concatenate([head[...], kern_ref[:, LANES:tile]], axis=1)
        else:
            kern = kern_ref[:, at : at + tile]
        add(
            slice(at, at + tile),
            lax.dot_general(kern, resid[...], TN, preferred_element_type=F32),
        )


def gradient_scratch(n, c_dim):
    return [pltpu.VMEM((n, c_dim), BF16), pltpu.VMEM((n, LANES), BF16)]


def half_kernel(
    core_ref,
    blk_ref,
    kern_ref,
    got_ref,
    eig_ref,
    scale_ref,
    targets_ref,
    w_ref,
    pred_ref,
    out_ref,
    resid,
    head,
):
    step = scale_ref[:, LANES + 32 :]

    def add(rows, product):
        out_ref[rows, :] = w_ref[rows, :] - step * product

    gradient(
        core_ref[0],
        blk_ref[0],
        kern_ref,
        got_ref,
        eig_ref,
        scale_ref,
        targets_ref,
        pred_ref,
        resid,
        head,
        512,
        add,
    )


def half_step(core, blk, kern, got, eig, scale, targets, weights):
    n, count = kern.shape
    c_dim = targets.shape[1]
    smem = pl.BlockSpec(memory_space=pltpu.SMEM)
    vmem = pl.BlockSpec(memory_space=pltpu.VMEM)
    return pl.pallas_call(
        half_kernel,
        in_specs=[smem] * 2 + [vmem] * 6,
        out_shape=(
            jax.ShapeDtypeStruct((HALF, c_dim), F32),
            jax.ShapeDtypeStruct((count, c_dim), F32),
        ),
        scratch_shapes=gradient_scratch(n, c_dim),
        compiler_params=params(16),
        cost_estimate=pl.CostEstimate(
            flops=20 * n * count * c_dim, bytes_accessed=4 << 20, transcendentals=0
        ),
        name="half_step",
    )(core, blk, kern, got, eig, scale, targets, weights)


def step_kernel(
    core_ref,
    blk_ref,
    kern_ref,
    got_ref,
    eig_ref,
    scale_ref,
    targets_ref,
    base_ref,
    own_ref,
    pred_ref,
    out_ref,
    resid,
    head,
    other,
    new,
    sem,
    pred_sem,
):
    core = core_ref[0]
    own_copy = pltpu.make_async_copy(
        own_ref, pred_ref.at[pl.ds(pl.multiple_of(core * HALF, HALF), HALF)], pred_sem.at[0]
    )
    own_copy.start()
    step = scale_ref[:, LANES + 32 :]
    copies = []

    def add(rows, product):
        new[rows, :] = base_ref[rows, :] - step * product
        k = len(copies)
        copies.append(pltpu.make_async_copy(new.at[rows], out_ref.at[rows], sem.at[k]))
        copies[k].start()

    gradient(
        1 - core,
        blk_ref[0],
        kern_ref,
        got_ref,
        eig_ref,
        scale_ref,
        targets_ref,
        other,
        resid,
        head,
        256,
        add,
    )
    other_copy = pltpu.make_async_copy(
        other, pred_ref.at[pl.ds(pl.multiple_of((1 - core) * HALF, HALF), HALF)], pred_sem.at[1]
    )
    other_copy.start()
    own_copy.wait()
    for copy in copies:
        copy.wait()
    other_copy.wait()


def take_step(core, blk, kern, got, eig, scale, targets, base, own):
    n, count = kern.shape
    c_dim = base.shape[1]
    smem = pl.BlockSpec(memory_space=pltpu.SMEM)
    vmem = pl.BlockSpec(memory_space=pltpu.VMEM)
    hbm = pl.BlockSpec(memory_space=pltpu.HBM)
    return pl.pallas_call(
        step_kernel,
        in_specs=[smem] * 2 + [vmem] * 7,
        out_specs=[hbm] * 2,
        out_shape=(
            jax.ShapeDtypeStruct(targets.shape, F32),
            jax.ShapeDtypeStruct(base.shape, F32),
        ),
        scratch_shapes=gradient_scratch(n, c_dim)
        + [
            pltpu.VMEM((HALF, c_dim), F32),
            pltpu.VMEM(base.shape, F32),
            pltpu.SemaphoreType.DMA((4,)),
            pltpu.SemaphoreType.DMA((2,)),
        ],
        compiler_params=params(16),
        cost_estimate=pl.CostEstimate(
            flops=2 * n * count * c_dim, bytes_accessed=8 << 20, transcendentals=0
        ),
        name="take_step",
    )(core, blk, kern, got, eig, scale, targets, base, own)


def sq_norm(rows):
    return jnp.sum(rows.astype(F32) ** 2, axis=1) * scale_of(rows.shape[1])


def swap_cores(value):
    return lax.ppermute(value, "c", [(0, 1), (1, 0)])


def local(batch, targets, centers, weights, eigvec, eig_scale, step):
    core = lax.axis_index("c").reshape(1)
    sub = lax.axis_index(SUB_AXES).reshape(1)
    blk = lax.axis_index(BLK).reshape(1)
    n, d = BLOCKS * HALF, batch.shape[1]

    first = lax.all_to_all(fan(core, sub, blk, batch), BLK, 0, 0, tiled=True).reshape(n, d)
    first, held, to_split = lax.optimization_barrier((first, centers, weights))
    second = swap_cores(first)
    cs = sq_norm(held)[None, :]
    count, c_dim = weights.shape
    extra = (
        jax.ShapeDtypeStruct((3 * count, c_dim), BF16),
        jax.ShapeDtypeStruct((HALF, 2 * LANES), F32),
    )
    sent, kern_first, weights3, eig = terms(
        first_kernel, first, held, cs, to_split, eigvec, extra
    )
    kept, kern_second = terms(second_kernel, second, held, cs, weights3, eig)
    coded = code(kept, swap_cores(sent)).astype(F16)

    got = lax.all_to_all(coded, NEAR, 0, 0, tiled=True).astype(F32)
    partial = recode(got).astype(F16)
    partial = jnp.broadcast_to(partial[None], (FAR_SIZE,) + partial.shape)
    far = lax.all_to_all(partial, FAR, 0, 0, tiled=True).astype(F32)

    packed = pack(core, sub, blk, far, targets).astype(F16)
    got_second = lax.all_to_all(packed, NEAR, 0, 0, tiled=True)
    got_first = swap_cores(got_second)
    scale = jnp.concatenate([eig_scale, step])[None, :]
    own, base = half_step(
        core, blk, kern_second, got_second.astype(F32), eig, scale, targets, weights
    )
    return take_step(
        core, blk, kern_first, got_first.astype(F32), eig, scale, targets, base, own
    )


def solution(mesh):
    fine = Mesh(mesh.devices.reshape(2, 4, 4, 2, 2, 2), AXES)
    return jax.shard_map(
        local,
        mesh=fine,
        in_specs=(P(BLK, None), P(BLK, None), ALL, ALL, ALL, P(), P()),
        out_specs=(P(BLK, None), ALL),
        check_vma=False,
    )
```

```python
import math

import jax
import jax.numpy as jnp
from jax import lax
from jax.experimental import pallas as pl
from jax.experimental.pallas import tpu as pltpu
from jax.sharding import Mesh, PartitionSpec as P

AXES = ("xl", "y", "zh", "zl", "xh", "c")
BLK = ("xl", "y")
SUB_AXES = ("xh", "zl")
NEAR = ("xh", "xl", "zl", "y")
FAR = "zh"
ALL = P(AXES, None)
F32 = jnp.float32
BF16 = jnp.bfloat16
F16 = jnp.float16
NT = (((1,), (1,)), ((), ()))
NN = (((1,), (0,)), ((), ()))
TN = (((0,), (0,)), ((), ()))

HALF = 64
BLOCKS = 8
SUB = 16
SUBS = 32
PER_BLOCK = HALF // SUB
LANES = 128
VALUE = 4 * SUB
MAIN = VALUE + SUB
CODED = MAIN + 8
FAR_SIZE = 4


def slot(blk, sub):
    return sub // 2 * 16 + blk // 4 * 8 + sub % 2 * 4 + blk % 4


def params(mib):
    return pltpu.CompilerParams(vmem_limit_bytes=mib << 20)


def split(value):
    high = value.astype(BF16)
    return high, (value - high.astype(F32)).astype(BF16)


def dot3(a, b, dims):
    a_hi, a_lo = split(a)
    b_hi, b_lo = split(b)

    def one(x, y):
        return lax.dot_general(x, y, dims, preferred_element_type=F32)

    return one(a_hi, b_hi) + one(a_hi, b_lo) + one(a_lo, b_hi)


def widen(eig):
    return jnp.concatenate([eig[:, :LANES]] + [eig[:, LANES:]] * 4, axis=1)


def lane_group(shape):
    return lax.broadcasted_iota(jnp.int32, shape, len(shape) - 1) // 32


def scale_of(features):
    return 4.0 / features * math.log2(math.e)


def fan_kernel(core_ref, sub_ref, blk_ref, rows_ref, out_ref):
    rows = rows_ref[...]
    for b in range(BLOCKS):
        out_ref[b] = rows


def fan(core, sub, blk, batch):
    d = batch.shape[1]
    return pl.pallas_call(
        fan_kernel,
        grid_spec=pltpu.PrefetchScalarGridSpec(
            num_scalar_prefetch=3,
            grid=(1,),
            in_specs=[pl.BlockSpec((HALF, d), lambda i, core, sub, blk: (1 - core[0], 0))],
            out_specs=pl.BlockSpec((BLOCKS, HALF, d), lambda i, core, sub, blk: (0, 0, 0)),
        ),
        out_shape=jax.ShapeDtypeStruct((BLOCKS, HALF, d), batch.dtype),
        compiler_params=params(8),
        name="fan",
    )(core, sub, blk, batch)


def terms_body(rows_ref, cen_ref, cs_ref, eig, weights3, out_ref, kern_ref, kern3):
    n, d = rows_ref.shape
    count = cen_ref.shape[0]
    tile = 512
    scale = scale_of(d)
    rows = rows_ref[...]
    wide = rows.astype(F32)
    rs = jnp.sum(wide * wide, axis=1, keepdims=True) * scale
    for at in range(0, count, tile):
        cols = slice(at, at + tile)
        cross = lax.dot_general(rows, cen_ref[cols, :], NT, preferred_element_type=F32)
        kern = jnp.exp2(cross * (2.0 * scale) - rs - cs_ref[:, cols])
        high, low = split(kern)
        kern3[:, at : at + tile] = high
        kern3[:, count + at : count + at + tile] = high
        kern_ref[:, cols] = high
        kern3[:, 2 * count + at : 2 * count + at + tile] = low
        if at == 0:
            coef = dot3(kern[:, :HALF], eig, NN)
            group = lane_group((8, LANES))
            for b in range(SUBS):
                block = coef[b * SUB : (b + 1) * SUB]
                at_b = slot(b // PER_BLOCK, b % PER_BLOCK)
                out_ref[at_b, VALUE:MAIN, :] = block[:, :LANES]
                tail = block[:, LANES:]
                out_ref[at_b, MAIN:CODED, :] = jnp.where(
                    group == 0, tail[:8], jnp.where(group == 1, tail[8:], 0.0)
                )
    value = lax.dot_general(kern3[...], weights3(), NN, preferred_element_type=F32)
    for b in range(SUBS):
        at_b = slot(b // PER_BLOCK, b % PER_BLOCK)
        for j in range(4):
            out_ref[at_b, j * SUB : (j + 1) * SUB, :] = value[
                b * SUB : (b + 1) * SUB, j * LANES : (j + 1) * LANES
            ]


def first_kernel(rows_ref, cen_ref, cs_ref, w_ref, e_ref, out_ref, kern_ref, w3_ref, e_out, kern3):
    eig = widen(e_ref[...])
    e_out[...] = eig

    def weights3():
        count = w_ref.shape[0]
        high, low = split(w_ref[...])
        w3_ref[:count] = high
        w3_ref[count : 2 * count] = low
        w3_ref[2 * count :] = high
        return w3_ref[...]

    terms_body(rows_ref, cen_ref, cs_ref, eig, weights3, out_ref, kern_ref, kern3)


def second_kernel(rows_ref, cen_ref, cs_ref, w3_ref, e_ref, out_ref, kern_ref, kern3):
    terms_body(
        rows_ref, cen_ref, cs_ref, e_ref[...], lambda: w3_ref[...], out_ref, kern_ref, kern3
    )


def terms(kernel, rows, centers, cs, weights, eig, extra=()):
    n, d = rows.shape
    count = centers.shape[0]
    c_dim = weights.shape[1]
    return pl.pallas_call(
        kernel,
        out_shape=(
            jax.ShapeDtypeStruct((SUBS, CODED, LANES), F32),
            jax.ShapeDtypeStruct((n, count), BF16),
        )
        + extra,
        scratch_shapes=[pltpu.VMEM((n, 3 * count), BF16)],
        compiler_params=params(24),
        cost_estimate=pl.CostEstimate(
            flops=20 * n * count * (d + 3 * c_dim), bytes_accessed=6 << 20, transcendentals=n * count
        ),
        name="terms",
    )(rows, centers, cs, weights, eig)


def scaled(part):
    top = jnp.max(jnp.abs(part), axis=(0, 1), keepdims=True)
    power = jnp.ceil(jnp.log2(jnp.maximum(top, 1e-30)))
    return part * jnp.exp2(14.0 - power), power


def with_powers(coef, value_power, coef_power):
    group = lane_group((8, LANES))
    powers = jnp.where(group == 2, value_power, coef_power)
    tile = jnp.where(group < 2, coef[SUB:], powers)
    return coef[:SUB], tile


def unscale(ref, b):
    value = jnp.exp2(ref[b, MAIN : MAIN + 1, 64:65] - 14.0)
    coef = jnp.exp2(ref[b, MAIN : MAIN + 1, 96:97] - 14.0)
    return value, coef


def sum_blocks(ref):
    value = jnp.zeros((VALUE, LANES), F32)
    main = jnp.zeros((SUB, LANES), F32)
    tile = jnp.zeros((8, LANES), F32)
    for b in range(ref.shape[0]):
        value_scale, coef_scale = unscale(ref, b)
        value += ref[b, :VALUE, :] * value_scale
        main += ref[b, VALUE:MAIN, :] * coef_scale
        tile += ref[b, MAIN:CODED, :] * coef_scale
    tile = jnp.where(lane_group((8, LANES)) < 2, tile, 0.0)
    return value, jnp.concatenate([main, tile], axis=0)


def code_kernel(a_ref, b_ref, out_ref):
    for b in range(SUBS):
        total = a_ref[b] + b_ref[b]
        value, value_power = scaled(total[:VALUE])
        coef, coef_power = scaled(total[VALUE:])
        main, tile = with_powers(coef, value_power, coef_power)
        out_ref[b, :VALUE, :] = value
        out_ref[b, VALUE:MAIN, :] = main
        out_ref[b, MAIN:CODED, :] = tile


def code(a, b):
    return pl.pallas_call(
        code_kernel,
        out_shape=jax.ShapeDtypeStruct((SUBS, CODED, LANES), F32),
        compiler_params=params(12),
        name="code",
    )(a, b)


def recode_kernel(x_ref, out_ref):
    value, coef = sum_blocks(x_ref)
    value, value_power = scaled(value)
    coef, coef_power = scaled(coef)
    main, tile = with_powers(coef, value_power, coef_power)
    out_ref[:VALUE, :] = value
    out_ref[VALUE:MAIN, :] = main
    out_ref[MAIN:CODED, :] = tile


def recode(x):
    return pl.pallas_call(
        recode_kernel,
        out_shape=jax.ShapeDtypeStruct((CODED, LANES), F32),
        compiler_params=params(12),
        name="recode",
    )(x)


def pack_kernel(core_ref, sub_ref, blk_ref, x_ref, targets_ref, out_ref):
    value, coef = sum_blocks(x_ref)
    row = pl.multiple_of(core_ref[0] * HALF + sub_ref[0] * SUB, SUB)
    resid = []
    for j in range(4):
        target = targets_ref[pl.ds(row, SUB), j * LANES : (j + 1) * LANES]
        resid.append(value[j * SUB : (j + 1) * SUB] - target)
    resid, resid_power = scaled(jnp.concatenate(resid, axis=0))
    value, value_power = scaled(value)
    coef, coef_power = scaled(coef)
    main, tile = with_powers(coef, resid_power, coef_power)
    for b in range(SUBS):
        out_ref[b, :VALUE, :] = resid
        out_ref[b, VALUE:MAIN, :] = main
        out_ref[b, MAIN:CODED, :] = tile
    _, tile = with_powers(coef, value_power, coef_power)
    for h in range(PER_BLOCK):
        b = slot(blk_ref[0], h)
        out_ref[b, :VALUE, :] = value
        out_ref[b, MAIN:CODED, :] = tile


def pack(core, sub, blk, x, targets):
    smem = pl.BlockSpec(memory_space=pltpu.SMEM)
    vmem = pl.BlockSpec(memory_space=pltpu.VMEM)
    return pl.pallas_call(
        pack_kernel,
        in_specs=[smem] * 3 + [vmem] * 2,
        out_shape=jax.ShapeDtypeStruct((SUBS, CODED, LANES), F32),
        compiler_params=params(12),
        name="pack",
    )(core, sub, blk, x, targets)


def gradient(
    half, blk, kern_ref, got_ref, eig_ref, scale_ref, targets_ref, pred_ref, resid, head, tile, add
):
    count = kern_ref.shape[1]
    group = lane_group((8, LANES))
    coefs = []
    for b in range(SUBS):
        at_b = slot(b // PER_BLOCK, b % PER_BLOCK)
        value_scale, coef_scale = unscale(got_ref, at_b)
        for j in range(4):
            resid[b * SUB : (b + 1) * SUB, j * LANES : (j + 1) * LANES] = (
                got_ref[at_b, j * SUB : (j + 1) * SUB, :] * value_scale
            ).astype(BF16)
        main = got_ref[at_b, VALUE:MAIN, :] * coef_scale
        tile_rows = got_ref[at_b, MAIN:CODED, :] * coef_scale
        tails = [jnp.where(group == t, tile_rows, 0.0) for t in range(2)]
        coefs.append(jnp.concatenate([main, jnp.concatenate(tails, axis=0)], axis=1).astype(BF16))
    for h in range(PER_BLOCK):
        b = blk * PER_BLOCK + h
        at_b = slot(blk, h)
        value_scale, _ = unscale(got_ref, at_b)
        row = pl.multiple_of(half * HALF + h * SUB, SUB)
        for j in range(4):
            lanes = slice(j * LANES, (j + 1) * LANES)
            value = got_ref[at_b, j * SUB : (j + 1) * SUB, :] * value_scale
            pred_ref[h * SUB : (h + 1) * SUB, lanes] = value
            target = targets_ref[pl.ds(row, SUB), lanes]
            resid[pl.ds(pl.multiple_of(b * SUB, SUB), SUB), lanes] = (value - target).astype(BF16)
    coef = jnp.concatenate(coefs, axis=0)
    corr = jnp.zeros((coef.shape[0], HALF), F32)
    for part in split(eig_ref[...] * widen(scale_ref[:, : LANES + 32])):
        corr += lax.dot_general(coef, part, NT, preferred_element_type=F32)
    head[...] = kern_ref[:, :LANES]
    head[:, :HALF] = (kern_ref[:, :HALF].astype(F32) - corr).astype(BF16)
    for at in [*range(tile, count, tile), 0]:
        if at == 0:
            kern = jnp.concatenate([head[...], kern_ref[:, LANES:tile]], axis=1)
        else:
            kern = kern_ref[:, at : at + tile]
        add(
            slice(at, at + tile),
            lax.dot_general(kern, resid[...], TN, preferred_element_type=F32),
        )


def gradient_scratch(n, c_dim):
    return [pltpu.VMEM((n, c_dim), BF16), pltpu.VMEM((n, LANES), BF16)]


def half_kernel(
    core_ref,
    blk_ref,
    kern_ref,
    got_ref,
    eig_ref,
    scale_ref,
    targets_ref,
    w_ref,
    pred_ref,
    out_ref,
    resid,
    head,
):
    step = scale_ref[:, LANES + 32 :]

    def add(rows, product):
        out_ref[rows, :] = w_ref[rows, :] - step * product

    gradient(
        core_ref[0],
        blk_ref[0],
        kern_ref,
        got_ref,
        eig_ref,
        scale_ref,
        targets_ref,
        pred_ref,
        resid,
        head,
        512,
        add,
    )


def half_step(core, blk, kern, got, eig, scale, targets, weights):
    n, count = kern.shape
    c_dim = targets.shape[1]
    smem = pl.BlockSpec(memory_space=pltpu.SMEM)
    vmem = pl.BlockSpec(memory_space=pltpu.VMEM)
    return pl.pallas_call(
        half_kernel,
        in_specs=[smem] * 2 + [vmem] * 6,
        out_shape=(
            jax.ShapeDtypeStruct((HALF, c_dim), F32),
            jax.ShapeDtypeStruct((count, c_dim), F32),
        ),
        scratch_shapes=gradient_scratch(n, c_dim),
        compiler_params=params(16),
        cost_estimate=pl.CostEstimate(
            flops=20 * n * count * c_dim, bytes_accessed=4 << 20, transcendentals=0
        ),
        name="half_step",
    )(core, blk, kern, got, eig, scale, targets, weights)


def step_kernel(
    core_ref,
    blk_ref,
    kern_ref,
    got_ref,
    eig_ref,
    scale_ref,
    targets_ref,
    base_ref,
    own_ref,
    pred_ref,
    out_ref,
    resid,
    head,
    other,
    new,
    sem,
    pred_sem,
):
    core = core_ref[0]
    own_copy = pltpu.make_async_copy(
        own_ref, pred_ref.at[pl.ds(pl.multiple_of(core * HALF, HALF), HALF)], pred_sem.at[0]
    )
    own_copy.start()
    step = scale_ref[:, LANES + 32 :]
    copies = []

    def add(rows, product):
        new[rows, :] = base_ref[rows, :] - step * product
        k = len(copies)
        copies.append(pltpu.make_async_copy(new.at[rows], out_ref.at[rows], sem.at[k]))
        copies[k].start()

    gradient(
        1 - core,
        blk_ref[0],
        kern_ref,
        got_ref,
        eig_ref,
        scale_ref,
        targets_ref,
        other,
        resid,
        head,
        256,
        add,
    )
    other_copy = pltpu.make_async_copy(
        other, pred_ref.at[pl.ds(pl.multiple_of((1 - core) * HALF, HALF), HALF)], pred_sem.at[1]
    )
    other_copy.start()
    own_copy.wait()
    for copy in copies:
        copy.wait()
    other_copy.wait()


def take_step(core, blk, kern, got, eig, scale, targets, base, own):
    n, count = kern.shape
    c_dim = base.shape[1]
    smem = pl.BlockSpec(memory_space=pltpu.SMEM)
    vmem = pl.BlockSpec(memory_space=pltpu.VMEM)
    hbm = pl.BlockSpec(memory_space=pltpu.HBM)
    return pl.pallas_call(
        step_kernel,
        in_specs=[smem] * 2 + [vmem] * 7,
        out_specs=[hbm] * 2,
        out_shape=(
            jax.ShapeDtypeStruct(targets.shape, F32),
            jax.ShapeDtypeStruct(base.shape, F32),
        ),
        scratch_shapes=gradient_scratch(n, c_dim)
        + [
            pltpu.VMEM((HALF, c_dim), F32),
            pltpu.VMEM(base.shape, F32),
            pltpu.SemaphoreType.DMA((4,)),
            pltpu.SemaphoreType.DMA((2,)),
        ],
        compiler_params=params(16),
        cost_estimate=pl.CostEstimate(
            flops=2 * n * count * c_dim, bytes_accessed=8 << 20, transcendentals=0
        ),
        name="take_step",
    )(core, blk, kern, got, eig, scale, targets, base, own)


def sq_norm(rows):
    return jnp.sum(rows.astype(F32) ** 2, axis=1) * scale_of(rows.shape[1])


def swap_cores(value):
    return lax.ppermute(value, "c", [(0, 1), (1, 0)])


def local(batch, targets, centers, weights, eigvec, eig_scale, step):
    core = lax.axis_index("c").reshape(1)
    sub = lax.axis_index(SUB_AXES).reshape(1)
    blk = lax.axis_index(BLK).reshape(1)
    n, d = BLOCKS * HALF, batch.shape[1]

    first = lax.all_to_all(fan(core, sub, blk, batch), BLK, 0, 0, tiled=True).reshape(n, d)
    first, held, to_split = lax.optimization_barrier((first, centers, weights))
    second = swap_cores(first)
    cs = sq_norm(held)[None, :]
    count, c_dim = weights.shape
    extra = (
        jax.ShapeDtypeStruct((3 * count, c_dim), BF16),
        jax.ShapeDtypeStruct((HALF, 2 * LANES), F32),
    )
    sent, kern_first, weights3, eig = terms(
        first_kernel, first, held, cs, to_split, eigvec, extra
    )
    kept, kern_second = terms(second_kernel, second, held, cs, weights3, eig)
    coded = code(kept, swap_cores(sent)).astype(F16)

    got = lax.all_to_all(coded, NEAR, 0, 0, tiled=True).astype(F32)
    partial = recode(got).astype(F16)
    partial = jnp.broadcast_to(partial[None], (FAR_SIZE,) + partial.shape)
    far = lax.all_to_all(partial, FAR, 0, 0, tiled=True).astype(F32)

    packed = pack(core, sub, blk, far, targets).astype(F16)
    got_second = lax.all_to_all(packed, NEAR, 0, 0, tiled=True)
    got_first = swap_cores(got_second)
    scale = jnp.concatenate([eig_scale, step])[None, :]
    own, base = half_step(
        core, blk, kern_second, got_second.astype(F32), eig, scale, targets, weights
    )
    return take_step(
        core, blk, kern_first, got_first.astype(F32), eig, scale, targets, base, own
    )


def solution(mesh):
    fine = Mesh(mesh.devices.reshape(2, 4, 4, 2, 2, 2), AXES)
    return jax.shard_map(
        local,
        mesh=fine,
        in_specs=(P(BLK, None), P(BLK, None), ALL, ALL, ALL, P(), P()),
        out_specs=(P(BLK, None), ALL),
        check_vma=False,
    )
```

```python
import math

import jax
import jax.numpy as jnp
from jax import lax
from jax.experimental import pallas as pl
from jax.experimental.pallas import tpu as pltpu
from jax.sharding import Mesh, PartitionSpec as P

AXES = ("xl", "y", "zh", "zl", "xh", "c")
BLK = ("xl", "y")
SUB_AXES = ("xh", "zl")
NEAR = ("xh", "xl", "zl", "y")
FAR = "zh"
ALL = P(AXES, None)
F32 = jnp.float32
BF16 = jnp.bfloat16
F16 = jnp.float16
NT = (((1,), (1,)), ((), ()))
NN = (((1,), (0,)), ((), ()))
TN = (((0,), (0,)), ((), ()))

HALF = 64
BLOCKS = 8
SUB = 16
SUBS = 32
PER_BLOCK = HALF // SUB
LANES = 128
VALUE = 4 * SUB
MAIN = VALUE + SUB
CODED = MAIN + 8
FAR_SIZE = 4


def slot(blk, sub):
    return sub // 2 * 16 + blk // 4 * 8 + sub % 2 * 4 + blk % 4


def params(mib):
    return pltpu.CompilerParams(vmem_limit_bytes=mib << 20)


def split(value):
    high = value.astype(BF16)
    return high, (value - high.astype(F32)).astype(BF16)


def dot3(a, b, dims):
    a_hi, a_lo = split(a)
    b_hi, b_lo = split(b)

    def one(x, y):
        return lax.dot_general(x, y, dims, preferred_element_type=F32)

    return one(a_hi, b_hi) + one(a_hi, b_lo) + one(a_lo, b_hi)


def widen(eig):
    return jnp.concatenate([eig[:, :LANES]] + [eig[:, LANES:]] * 4, axis=1)


def lane_group(shape):
    return lax.broadcasted_iota(jnp.int32, shape, len(shape) - 1) // 32


def scale_of(features):
    return 4.0 / features * math.log2(math.e)


def fan_kernel(core_ref, sub_ref, blk_ref, rows_ref, out_ref):
    rows = rows_ref[...]
    for b in range(BLOCKS):
        out_ref[b] = rows


def fan(core, sub, blk, batch):
    d = batch.shape[1]
    return pl.pallas_call(
        fan_kernel,
        grid_spec=pltpu.PrefetchScalarGridSpec(
            num_scalar_prefetch=3,
            grid=(1,),
            in_specs=[pl.BlockSpec((HALF, d), lambda i, core, sub, blk: (1 - core[0], 0))],
            out_specs=pl.BlockSpec((BLOCKS, HALF, d), lambda i, core, sub, blk: (0, 0, 0)),
        ),
        out_shape=jax.ShapeDtypeStruct((BLOCKS, HALF, d), batch.dtype),
        compiler_params=params(8),
        name="fan",
    )(core, sub, blk, batch)


def terms_body(rows_ref, cen_ref, cs_ref, eig, weights3, out_ref, kern_ref, kern3):
    n, d = rows_ref.shape
    count = cen_ref.shape[0]
    tile = 512
    scale = scale_of(d)
    rows = rows_ref[...]
    wide = rows.astype(F32)
    rs = jnp.sum(wide * wide, axis=1, keepdims=True) * scale
    for at in range(0, count, tile):
        cols = slice(at, at + tile)
        cross = lax.dot_general(rows, cen_ref[cols, :], NT, preferred_element_type=F32)
        kern = jnp.exp2(cross * (2.0 * scale) - rs - cs_ref[:, cols])
        high, low = split(kern)
        kern3[:, at : at + tile] = high
        kern3[:, count + at : count + at + tile] = high
        kern_ref[:, cols] = high
        kern3[:, 2 * count + at : 2 * count + at + tile] = low
        if at == 0:
            coef = dot3(kern[:, :HALF], eig, NN)
            group = lane_group((8, LANES))
            for b in range(SUBS):
                block = coef[b * SUB : (b + 1) * SUB]
                at_b = slot(b // PER_BLOCK, b % PER_BLOCK)
                out_ref[at_b, VALUE:MAIN, :] = block[:, :LANES]
                tail = block[:, LANES:]
                out_ref[at_b, MAIN:CODED, :] = jnp.where(
                    group == 0, tail[:8], jnp.where(group == 1, tail[8:], 0.0)
                )
    value = lax.dot_general(kern3[...], weights3(), NN, preferred_element_type=F32)
    for b in range(SUBS):
        at_b = slot(b // PER_BLOCK, b % PER_BLOCK)
        for j in range(4):
            out_ref[at_b, j * SUB : (j + 1) * SUB, :] = value[
                b * SUB : (b + 1) * SUB, j * LANES : (j + 1) * LANES
            ]


def first_kernel(rows_ref, cen_ref, cs_ref, w_ref, e_ref, out_ref, kern_ref, w3_ref, e_out, kern3):
    eig = widen(e_ref[...])
    e_out[...] = eig

    def weights3():
        count = w_ref.shape[0]
        high, low = split(w_ref[...])
        w3_ref[:count] = high
        w3_ref[count : 2 * count] = low
        w3_ref[2 * count :] = high
        return w3_ref[...]

    terms_body(rows_ref, cen_ref, cs_ref, eig, weights3, out_ref, kern_ref, kern3)


def second_kernel(rows_ref, cen_ref, cs_ref, w3_ref, e_ref, out_ref, kern_ref, kern3):
    terms_body(
        rows_ref, cen_ref, cs_ref, e_ref[...], lambda: w3_ref[...], out_ref, kern_ref, kern3
    )


def terms(kernel, rows, centers, cs, weights, eig, extra=()):
    n, d = rows.shape
    count = centers.shape[0]
    c_dim = weights.shape[1]
    return pl.pallas_call(
        kernel,
        out_shape=(
            jax.ShapeDtypeStruct((SUBS, CODED, LANES), F32),
            jax.ShapeDtypeStruct((n, count), BF16),
        )
        + extra,
        scratch_shapes=[pltpu.VMEM((n, 3 * count), BF16)],
        compiler_params=params(24),
        cost_estimate=pl.CostEstimate(
            flops=20 * n * count * (d + 3 * c_dim), bytes_accessed=6 << 20, transcendentals=n * count
        ),
        name="terms",
    )(rows, centers, cs, weights, eig)


def scaled(part):
    top = jnp.max(jnp.abs(part), axis=(0, 1), keepdims=True)
    power = jnp.ceil(jnp.log2(jnp.maximum(top, 1e-30)))
    return part * jnp.exp2(14.0 - power), power


def with_powers(coef, value_power, coef_power):
    group = lane_group((8, LANES))
    powers = jnp.where(group == 2, value_power, coef_power)
    tile = jnp.where(group < 2, coef[SUB:], powers)
    return coef[:SUB], tile


def unscale(ref, b):
    value = jnp.exp2(ref[b, MAIN : MAIN + 1, 64:65] - 14.0)
    coef = jnp.exp2(ref[b, MAIN : MAIN + 1, 96:97] - 14.0)
    return value, coef


def unscale_all(ref):
    powers = jnp.concatenate([ref[b, MAIN : MAIN + 1, :] for b in range(ref.shape[0])], axis=0)
    shape = powers.shape
    value = jnp.exp2(jnp.broadcast_to(powers[:, 64:65], shape) - 14.0)
    coef = jnp.exp2(jnp.broadcast_to(powers[:, 96:97], shape) - 14.0)
    return [(value[b : b + 1], coef[b : b + 1]) for b in range(shape[0])]


def sum_blocks(ref):
    value = jnp.zeros((VALUE, LANES), F32)
    main = jnp.zeros((SUB, LANES), F32)
    tile = jnp.zeros((8, LANES), F32)
    scales = unscale_all(ref)
    for b in range(ref.shape[0]):
        value_scale, coef_scale = scales[b]
        value += ref[b, :VALUE, :] * value_scale
        main += ref[b, VALUE:MAIN, :] * coef_scale
        tile += ref[b, MAIN:CODED, :] * coef_scale
    tile = jnp.where(lane_group((8, LANES)) < 2, tile, 0.0)
    return value, jnp.concatenate([main, tile], axis=0)


def code_kernel(a_ref, b_ref, out_ref):
    for b in range(SUBS):
        total = a_ref[b] + b_ref[b]
        value, value_power = scaled(total[:VALUE])
        coef, coef_power = scaled(total[VALUE:])
        main, tile = with_powers(coef, value_power, coef_power)
        out_ref[b, :VALUE, :] = value
        out_ref[b, VALUE:MAIN, :] = main
        out_ref[b, MAIN:CODED, :] = tile


def code(a, b):
    return pl.pallas_call(
        code_kernel,
        out_shape=jax.ShapeDtypeStruct((SUBS, CODED, LANES), F32),
        compiler_params=params(12),
        name="code",
    )(a, b)


def recode_kernel(x_ref, out_ref):
    value, coef = sum_blocks(x_ref)
    value, value_power = scaled(value)
    coef, coef_power = scaled(coef)
    main, tile = with_powers(coef, value_power, coef_power)
    out_ref[:VALUE, :] = value
    out_ref[VALUE:MAIN, :] = main
    out_ref[MAIN:CODED, :] = tile


def recode(x):
    return pl.pallas_call(
        recode_kernel,
        out_shape=jax.ShapeDtypeStruct((CODED, LANES), F32),
        compiler_params=params(12),
        name="recode",
    )(x)


def pack_kernel(core_ref, sub_ref, blk_ref, x_ref, targets_ref, out_ref):
    value, coef = sum_blocks(x_ref)
    row = pl.multiple_of(core_ref[0] * HALF + sub_ref[0] * SUB, SUB)
    resid = []
    for j in range(4):
        target = targets_ref[pl.ds(row, SUB), j * LANES : (j + 1) * LANES]
        resid.append(value[j * SUB : (j + 1) * SUB] - target)
    resid, resid_power = scaled(jnp.concatenate(resid, axis=0))
    value, value_power = scaled(value)
    coef, coef_power = scaled(coef)
    main, tile = with_powers(coef, resid_power, coef_power)
    for b in range(SUBS):
        out_ref[b, :VALUE, :] = resid
        out_ref[b, VALUE:MAIN, :] = main
        out_ref[b, MAIN:CODED, :] = tile
    _, tile = with_powers(coef, value_power, coef_power)
    for h in range(PER_BLOCK):
        b = slot(blk_ref[0], h)
        out_ref[b, :VALUE, :] = value
        out_ref[b, MAIN:CODED, :] = tile


def pack(core, sub, blk, x, targets):
    smem = pl.BlockSpec(memory_space=pltpu.SMEM)
    vmem = pl.BlockSpec(memory_space=pltpu.VMEM)
    return pl.pallas_call(
        pack_kernel,
        in_specs=[smem] * 3 + [vmem] * 2,
        out_shape=jax.ShapeDtypeStruct((SUBS, CODED, LANES), F32),
        compiler_params=params(12),
        name="pack",
    )(core, sub, blk, x, targets)


def gradient(
    half, blk, kern_ref, got_ref, eig_ref, scale_ref, targets_ref, pred_ref, resid, head, tile, add
):
    count = kern_ref.shape[1]
    group = lane_group((8, LANES))
    coefs = []
    scales = unscale_all(got_ref)
    for b in range(SUBS):
        at_b = slot(b // PER_BLOCK, b % PER_BLOCK)
        value_scale, coef_scale = scales[at_b]
        for j in range(4):
            resid[b * SUB : (b + 1) * SUB, j * LANES : (j + 1) * LANES] = (
                got_ref[at_b, j * SUB : (j + 1) * SUB, :] * value_scale
            ).astype(BF16)
        main = got_ref[at_b, VALUE:MAIN, :] * coef_scale
        tile_rows = got_ref[at_b, MAIN:CODED, :] * coef_scale
        tails = [jnp.where(group == t, tile_rows, 0.0) for t in range(2)]
        coefs.append(jnp.concatenate([main, jnp.concatenate(tails, axis=0)], axis=1).astype(BF16))
    for h in range(PER_BLOCK):
        b = blk * PER_BLOCK + h
        at_b = slot(blk, h)
        value_scale, _ = unscale(got_ref, at_b)
        row = pl.multiple_of(half * HALF + h * SUB, SUB)
        for j in range(4):
            lanes = slice(j * LANES, (j + 1) * LANES)
            value = got_ref[at_b, j * SUB : (j + 1) * SUB, :] * value_scale
            pred_ref[h * SUB : (h + 1) * SUB, lanes] = value
            target = targets_ref[pl.ds(row, SUB), lanes]
            resid[pl.ds(pl.multiple_of(b * SUB, SUB), SUB), lanes] = (value - target).astype(BF16)
    coef = jnp.concatenate(coefs, axis=0)
    corr = jnp.zeros((coef.shape[0], HALF), F32)
    for part in split(eig_ref[...] * widen(scale_ref[:, : LANES + 32])):
        corr += lax.dot_general(coef, part, NT, preferred_element_type=F32)
    head[...] = kern_ref[:, :LANES]
    head[:, :HALF] = (kern_ref[:, :HALF].astype(F32) - corr).astype(BF16)
    for at in [*range(tile, count, tile), 0]:
        if at == 0:
            kern = head[...]
            if tile > LANES:
                kern = jnp.concatenate([kern, kern_ref[:, LANES:tile]], axis=1)
        else:
            kern = kern_ref[:, at : at + tile]
        add(
            slice(at, at + tile),
            lax.dot_general(kern, resid[...], TN, preferred_element_type=F32),
        )


def gradient_scratch(n, c_dim):
    return [pltpu.VMEM((n, c_dim), BF16), pltpu.VMEM((n, LANES), BF16)]


def half_kernel(
    core_ref,
    blk_ref,
    kern_ref,
    got_ref,
    eig_ref,
    scale_ref,
    targets_ref,
    w_ref,
    pred_ref,
    out_ref,
    resid,
    head,
):
    step = scale_ref[:, LANES + 32 :]

    def add(rows, product):
        out_ref[rows, :] = w_ref[rows, :] - step * product

    gradient(
        core_ref[0],
        blk_ref[0],
        kern_ref,
        got_ref,
        eig_ref,
        scale_ref,
        targets_ref,
        pred_ref,
        resid,
        head,
        512,
        add,
    )


def half_step(core, blk, kern, got, eig, scale, targets, weights):
    n, count = kern.shape
    c_dim = targets.shape[1]
    smem = pl.BlockSpec(memory_space=pltpu.SMEM)
    vmem = pl.BlockSpec(memory_space=pltpu.VMEM)
    return pl.pallas_call(
        half_kernel,
        in_specs=[smem] * 2 + [vmem] * 6,
        out_shape=(
            jax.ShapeDtypeStruct((HALF, c_dim), F32),
            jax.ShapeDtypeStruct((count, c_dim), F32),
        ),
        scratch_shapes=gradient_scratch(n, c_dim),
        compiler_params=params(16),
        cost_estimate=pl.CostEstimate(
            flops=20 * n * count * c_dim, bytes_accessed=4 << 20, transcendentals=0
        ),
        name="half_step",
    )(core, blk, kern, got, eig, scale, targets, weights)


def step_kernel(
    core_ref,
    blk_ref,
    kern_ref,
    got_ref,
    eig_ref,
    scale_ref,
    targets_ref,
    base_ref,
    own_ref,
    pred_ref,
    out_ref,
    resid,
    head,
    other,
    new,
    sem,
    pred_sem,
):
    core = core_ref[0]
    own_copy = pltpu.make_async_copy(
        own_ref, pred_ref.at[pl.ds(pl.multiple_of(core * HALF, HALF), HALF)], pred_sem.at[0]
    )
    own_copy.start()
    step = scale_ref[:, LANES + 32 :]
    copies = []

    def add(rows, product):
        new[rows, :] = base_ref[rows, :] - step * product
        k = len(copies)
        copies.append(pltpu.make_async_copy(new.at[rows], out_ref.at[rows], sem.at[k]))
        copies[k].start()

    gradient(
        1 - core,
        blk_ref[0],
        kern_ref,
        got_ref,
        eig_ref,
        scale_ref,
        targets_ref,
        other,
        resid,
        head,
        128,
        add,
    )
    other_copy = pltpu.make_async_copy(
        other, pred_ref.at[pl.ds(pl.multiple_of((1 - core) * HALF, HALF), HALF)], pred_sem.at[1]
    )
    other_copy.start()
    own_copy.wait()
    for copy in copies:
        copy.wait()
    other_copy.wait()


def take_step(core, blk, kern, got, eig, scale, targets, base, own):
    n, count = kern.shape
    c_dim = base.shape[1]
    smem = pl.BlockSpec(memory_space=pltpu.SMEM)
    vmem = pl.BlockSpec(memory_space=pltpu.VMEM)
    hbm = pl.BlockSpec(memory_space=pltpu.HBM)
    return pl.pallas_call(
        step_kernel,
        in_specs=[smem] * 2 + [vmem] * 7,
        out_specs=[hbm] * 2,
        out_shape=(
            jax.ShapeDtypeStruct(targets.shape, F32),
            jax.ShapeDtypeStruct(base.shape, F32),
        ),
        scratch_shapes=gradient_scratch(n, c_dim)
        + [
            pltpu.VMEM((HALF, c_dim), F32),
            pltpu.VMEM(base.shape, F32),
            pltpu.SemaphoreType.DMA((8,)),
            pltpu.SemaphoreType.DMA((2,)),
        ],
        compiler_params=params(16),
        cost_estimate=pl.CostEstimate(
            flops=2 * n * count * c_dim, bytes_accessed=8 << 20, transcendentals=0
        ),
        name="take_step",
    )(core, blk, kern, got, eig, scale, targets, base, own)


def sq_norm(rows):
    return jnp.sum(rows.astype(F32) ** 2, axis=1) * scale_of(rows.shape[1])


def swap_cores(value):
    return lax.ppermute(value, "c", [(0, 1), (1, 0)])


def local(batch, targets, centers, weights, eigvec, eig_scale, step):
    core = lax.axis_index("c").reshape(1)
    sub = lax.axis_index(SUB_AXES).reshape(1)
    blk = lax.axis_index(BLK).reshape(1)
    n, d = BLOCKS * HALF, batch.shape[1]

    first = lax.all_to_all(fan(core, sub, blk, batch), BLK, 0, 0, tiled=True).reshape(n, d)
    first, held, to_split = lax.optimization_barrier((first, centers, weights))
    second = swap_cores(first)
    cs = sq_norm(held)[None, :]
    count, c_dim = weights.shape
    extra = (
        jax.ShapeDtypeStruct((3 * count, c_dim), BF16),
        jax.ShapeDtypeStruct((HALF, 2 * LANES), F32),
    )
    sent, kern_first, weights3, eig = terms(
        first_kernel, first, held, cs, to_split, eigvec, extra
    )
    kept, kern_second = terms(second_kernel, second, held, cs, weights3, eig)
    coded = code(kept, swap_cores(sent)).astype(F16)

    got = lax.all_to_all(coded, NEAR, 0, 0, tiled=True).astype(F32)
    partial = recode(got).astype(F16)
    partial = jnp.broadcast_to(partial[None], (FAR_SIZE,) + partial.shape)
    far = lax.all_to_all(partial, FAR, 0, 0, tiled=True).astype(F32)

    packed = pack(core, sub, blk, far, targets).astype(F16)
    got_second = lax.all_to_all(packed, NEAR, 0, 0, tiled=True)
    got_first = swap_cores(got_second)
    scale = jnp.concatenate([eig_scale, step])[None, :]
    own, base = half_step(
        core, blk, kern_second, got_second.astype(F32), eig, scale, targets, weights
    )
    return take_step(
        core, blk, kern_first, got_first.astype(F32), eig, scale, targets, base, own
    )


def solution(mesh):
    fine = Mesh(mesh.devices.reshape(2, 4, 4, 2, 2, 2), AXES)
    return jax.shard_map(
        local,
        mesh=fine,
        in_specs=(P(BLK, None), P(BLK, None), ALL, ALL, ALL, P(), P()),
        out_specs=(P(BLK, None), ALL),
        check_vma=False,
    )
```

```python
import math

import jax
import jax.numpy as jnp
from jax import lax
from jax.experimental import pallas as pl
from jax.experimental.pallas import tpu as pltpu
from jax.sharding import Mesh, PartitionSpec as P

AXES = ("xl", "y", "zh", "zl", "xh", "c")
BLK = ("xl", "y")
SUB_AXES = ("xh", "zl")
NEAR = ("xh", "xl", "zl", "y")
FAR = "zh"
ALL = P(AXES, None)
F32 = jnp.float32
BF16 = jnp.bfloat16
F16 = jnp.float16
NT = (((1,), (1,)), ((), ()))
NN = (((1,), (0,)), ((), ()))
TN = (((0,), (0,)), ((), ()))

HALF = 64
BLOCKS = 8
SUB = 16
SUBS = 32
PER_BLOCK = HALF // SUB
LANES = 128
VALUE = 4 * SUB
MAIN = VALUE + SUB
CODED = MAIN + 8
FAR_SIZE = 4


def slot(blk, sub):
    return sub // 2 * 16 + blk // 4 * 8 + sub % 2 * 4 + blk % 4


def params(mib):
    return pltpu.CompilerParams(vmem_limit_bytes=mib << 20)


def split(value):
    high = value.astype(BF16)
    return high, (value - high.astype(F32)).astype(BF16)


def dot3(a, b, dims):
    a_hi, a_lo = split(a)
    b_hi, b_lo = split(b)

    def one(x, y):
        return lax.dot_general(x, y, dims, preferred_element_type=F32)

    return one(a_hi, b_hi) + one(a_hi, b_lo) + one(a_lo, b_hi)


def widen(eig):
    return jnp.concatenate([eig[:, :LANES]] + [eig[:, LANES:]] * 4, axis=1)


def lane_group(shape):
    return lax.broadcasted_iota(jnp.int32, shape, len(shape) - 1) // 32


def scale_of(features):
    return 4.0 / features * math.log2(math.e)


def fan_kernel(core_ref, sub_ref, blk_ref, rows_ref, out_ref):
    rows = rows_ref[...]
    for b in range(BLOCKS):
        out_ref[b] = rows


def fan(core, sub, blk, batch):
    d = batch.shape[1]
    return pl.pallas_call(
        fan_kernel,
        grid_spec=pltpu.PrefetchScalarGridSpec(
            num_scalar_prefetch=3,
            grid=(1,),
            in_specs=[pl.BlockSpec((HALF, d), lambda i, core, sub, blk: (1 - core[0], 0))],
            out_specs=pl.BlockSpec((BLOCKS, HALF, d), lambda i, core, sub, blk: (0, 0, 0)),
        ),
        out_shape=jax.ShapeDtypeStruct((BLOCKS, HALF, d), batch.dtype),
        compiler_params=params(8),
        name="fan",
    )(core, sub, blk, batch)


def terms_body(rows_ref, cen_ref, cs_ref, eig, weights3, out_ref, kern_ref, kern3):
    n, d = rows_ref.shape
    count = cen_ref.shape[0]
    tile = 512
    scale = scale_of(d)
    rows = rows_ref[...]
    wide = rows.astype(F32)
    rs = jnp.sum(wide * wide, axis=1, keepdims=True) * scale
    for at in range(0, count, tile):
        cols = slice(at, at + tile)
        cross = lax.dot_general(rows, cen_ref[cols, :], NT, preferred_element_type=F32)
        kern = jnp.exp2(cross * (2.0 * scale) - rs - cs_ref[:, cols])
        high, low = split(kern)
        kern3[:, at : at + tile] = high
        kern3[:, count + at : count + at + tile] = high
        kern_ref[:, cols] = high
        kern3[:, 2 * count + at : 2 * count + at + tile] = low
        if at == 0:
            coef = jnp.zeros((n, eig.shape[1]), F32)
            for part in split(eig):
                coef += lax.dot_general(high[:, :HALF], part, NN, preferred_element_type=F32)
            group = lane_group((8, LANES))
            for b in range(SUBS):
                block = coef[b * SUB : (b + 1) * SUB]
                at_b = slot(b // PER_BLOCK, b % PER_BLOCK)
                out_ref[at_b, VALUE:MAIN, :] = block[:, :LANES]
                tail = block[:, LANES:]
                out_ref[at_b, MAIN:CODED, :] = jnp.where(
                    group == 0, tail[:8], jnp.where(group == 1, tail[8:], 0.0)
                )
    value = lax.dot_general(kern3[...], weights3(), NN, preferred_element_type=F32)
    for b in range(SUBS):
        at_b = slot(b // PER_BLOCK, b % PER_BLOCK)
        for j in range(4):
            out_ref[at_b, j * SUB : (j + 1) * SUB, :] = value[
                b * SUB : (b + 1) * SUB, j * LANES : (j + 1) * LANES
            ]


def first_kernel(rows_ref, cen_ref, cs_ref, w_ref, e_ref, out_ref, kern_ref, w3_ref, e_out, kern3):
    eig = widen(e_ref[...])
    e_out[...] = eig

    def weights3():
        count = w_ref.shape[0]
        high, low = split(w_ref[...])
        w3_ref[:count] = high
        w3_ref[count : 2 * count] = low
        w3_ref[2 * count :] = high
        return w3_ref[...]

    terms_body(rows_ref, cen_ref, cs_ref, eig, weights3, out_ref, kern_ref, kern3)


def second_kernel(rows_ref, cen_ref, cs_ref, w3_ref, e_ref, out_ref, kern_ref, kern3):
    terms_body(
        rows_ref, cen_ref, cs_ref, e_ref[...], lambda: w3_ref[...], out_ref, kern_ref, kern3
    )


def terms(kernel, rows, centers, cs, weights, eig, extra=()):
    n, d = rows.shape
    count = centers.shape[0]
    c_dim = weights.shape[1]
    return pl.pallas_call(
        kernel,
        out_shape=(
            jax.ShapeDtypeStruct((SUBS, CODED, LANES), F32),
            jax.ShapeDtypeStruct((n, count), BF16),
        )
        + extra,
        scratch_shapes=[pltpu.VMEM((n, 3 * count), BF16)],
        compiler_params=params(24),
        cost_estimate=pl.CostEstimate(
            flops=20 * n * count * (d + 3 * c_dim), bytes_accessed=6 << 20, transcendentals=n * count
        ),
        name="terms",
    )(rows, centers, cs, weights, eig)


def scaled(part):
    top = jnp.max(jnp.abs(part), axis=(0, 1), keepdims=True)
    power = jnp.ceil(jnp.log2(jnp.maximum(top, 1e-30)))
    return part * jnp.exp2(14.0 - power), power


def with_powers(coef, value_power, coef_power):
    group = lane_group((8, LANES))
    powers = jnp.where(group == 2, value_power, coef_power)
    tile = jnp.where(group < 2, coef[SUB:], powers)
    return coef[:SUB], tile


def unscale(ref, b):
    value = jnp.exp2(ref[b, MAIN : MAIN + 1, 64:65] - 14.0)
    coef = jnp.exp2(ref[b, MAIN : MAIN + 1, 96:97] - 14.0)
    return value, coef


def unscale_all(ref):
    powers = jnp.concatenate([ref[b, MAIN : MAIN + 1, :] for b in range(ref.shape[0])], axis=0)
    shape = powers.shape
    value = jnp.exp2(jnp.broadcast_to(powers[:, 64:65], shape) - 14.0)
    coef = jnp.exp2(jnp.broadcast_to(powers[:, 96:97], shape) - 14.0)
    return [(value[b : b + 1], coef[b : b + 1]) for b in range(shape[0])]


def sum_blocks(ref):
    value = jnp.zeros((VALUE, LANES), F32)
    main = jnp.zeros((SUB, LANES), F32)
    tile = jnp.zeros((8, LANES), F32)
    scales = unscale_all(ref)
    for b in range(ref.shape[0]):
        value_scale, coef_scale = scales[b]
        value += ref[b, :VALUE, :] * value_scale
        main += ref[b, VALUE:MAIN, :] * coef_scale
        tile += ref[b, MAIN:CODED, :] * coef_scale
    tile = jnp.where(lane_group((8, LANES)) < 2, tile, 0.0)
    return value, jnp.concatenate([main, tile], axis=0)


def code_kernel(a_ref, b_ref, out_ref):
    for b in range(SUBS):
        total = a_ref[b] + b_ref[b]
        value, value_power = scaled(total[:VALUE])
        coef, coef_power = scaled(total[VALUE:])
        main, tile = with_powers(coef, value_power, coef_power)
        out_ref[b, :VALUE, :] = value
        out_ref[b, VALUE:MAIN, :] = main
        out_ref[b, MAIN:CODED, :] = tile


def code(a, b):
    return pl.pallas_call(
        code_kernel,
        out_shape=jax.ShapeDtypeStruct((SUBS, CODED, LANES), F32),
        compiler_params=params(12),
        name="code",
    )(a, b)


def recode_kernel(x_ref, out_ref):
    value, coef = sum_blocks(x_ref)
    value, value_power = scaled(value)
    coef, coef_power = scaled(coef)
    main, tile = with_powers(coef, value_power, coef_power)
    out_ref[:VALUE, :] = value
    out_ref[VALUE:MAIN, :] = main
    out_ref[MAIN:CODED, :] = tile


def recode(x):
    return pl.pallas_call(
        recode_kernel,
        out_shape=jax.ShapeDtypeStruct((CODED, LANES), F32),
        compiler_params=params(12),
        name="recode",
    )(x)


def pack_kernel(core_ref, sub_ref, blk_ref, x_ref, targets_ref, out_ref):
    value, coef = sum_blocks(x_ref)
    row = pl.multiple_of(core_ref[0] * HALF + sub_ref[0] * SUB, SUB)
    resid = []
    for j in range(4):
        target = targets_ref[pl.ds(row, SUB), j * LANES : (j + 1) * LANES]
        resid.append(value[j * SUB : (j + 1) * SUB] - target)
    resid, resid_power = scaled(jnp.concatenate(resid, axis=0))
    value, value_power = scaled(value)
    coef, coef_power = scaled(coef)
    main, tile = with_powers(coef, resid_power, coef_power)
    for b in range(SUBS):
        out_ref[b, :VALUE, :] = resid
        out_ref[b, VALUE:MAIN, :] = main
        out_ref[b, MAIN:CODED, :] = tile
    _, tile = with_powers(coef, value_power, coef_power)
    for h in range(PER_BLOCK):
        b = slot(blk_ref[0], h)
        out_ref[b, :VALUE, :] = value
        out_ref[b, MAIN:CODED, :] = tile


def pack(core, sub, blk, x, targets):
    smem = pl.BlockSpec(memory_space=pltpu.SMEM)
    vmem = pl.BlockSpec(memory_space=pltpu.VMEM)
    return pl.pallas_call(
        pack_kernel,
        in_specs=[smem] * 3 + [vmem] * 2,
        out_shape=jax.ShapeDtypeStruct((SUBS, CODED, LANES), F32),
        compiler_params=params(12),
        name="pack",
    )(core, sub, blk, x, targets)


def gradient(
    half, blk, kern_ref, got_ref, eig_ref, scale_ref, targets_ref, pred_ref, resid, head, tile, add
):
    count = kern_ref.shape[1]
    group = lane_group((8, LANES))
    coefs = []
    scales = unscale_all(got_ref)
    for b in range(SUBS):
        at_b = slot(b // PER_BLOCK, b % PER_BLOCK)
        value_scale, coef_scale = scales[at_b]
        for j in range(4):
            resid[b * SUB : (b + 1) * SUB, j * LANES : (j + 1) * LANES] = (
                got_ref[at_b, j * SUB : (j + 1) * SUB, :] * value_scale
            ).astype(BF16)
        main = got_ref[at_b, VALUE:MAIN, :] * coef_scale
        tile_rows = got_ref[at_b, MAIN:CODED, :] * coef_scale
        tails = [jnp.where(group == t, tile_rows, 0.0) for t in range(2)]
        coefs.append(jnp.concatenate([main, jnp.concatenate(tails, axis=0)], axis=1).astype(BF16))
    for h in range(PER_BLOCK):
        b = blk * PER_BLOCK + h
        at_b = slot(blk, h)
        value_scale, _ = unscale(got_ref, at_b)
        row = pl.multiple_of(half * HALF + h * SUB, SUB)
        for j in range(4):
            lanes = slice(j * LANES, (j + 1) * LANES)
            value = got_ref[at_b, j * SUB : (j + 1) * SUB, :] * value_scale
            pred_ref[h * SUB : (h + 1) * SUB, lanes] = value
            target = targets_ref[pl.ds(row, SUB), lanes]
            resid[pl.ds(pl.multiple_of(b * SUB, SUB), SUB), lanes] = (value - target).astype(BF16)
    coef = jnp.concatenate(coefs, axis=0)
    corr = jnp.zeros((coef.shape[0], HALF), F32)
    for part in split(eig_ref[...] * widen(scale_ref[:, : LANES + 32])):
        corr += lax.dot_general(coef, part, NT, preferred_element_type=F32)
    head[...] = kern_ref[:, :LANES]
    head[:, :HALF] = (kern_ref[:, :HALF].astype(F32) - corr).astype(BF16)
    for at in [*range(tile, count, tile), 0]:
        if at == 0:
            kern = head[...]
            if tile > LANES:
                kern = jnp.concatenate([kern, kern_ref[:, LANES:tile]], axis=1)
        else:
            kern = kern_ref[:, at : at + tile]
        add(
            slice(at, at + tile),
            lax.dot_general(kern, resid[...], TN, preferred_element_type=F32),
        )


def gradient_scratch(n, c_dim):
    return [pltpu.VMEM((n, c_dim), BF16), pltpu.VMEM((n, LANES), BF16)]


def half_kernel(
    core_ref,
    blk_ref,
    kern_ref,
    got_ref,
    eig_ref,
    scale_ref,
    targets_ref,
    w_ref,
    pred_ref,
    out_ref,
    resid,
    head,
):
    step = scale_ref[:, LANES + 32 :]

    def add(rows, product):
        out_ref[rows, :] = w_ref[rows, :] - step * product

    gradient(
        core_ref[0],
        blk_ref[0],
        kern_ref,
        got_ref,
        eig_ref,
        scale_ref,
        targets_ref,
        pred_ref,
        resid,
        head,
        512,
        add,
    )


def half_step(core, blk, kern, got, eig, scale, targets, weights):
    n, count = kern.shape
    c_dim = targets.shape[1]
    smem = pl.BlockSpec(memory_space=pltpu.SMEM)
    vmem = pl.BlockSpec(memory_space=pltpu.VMEM)
    return pl.pallas_call(
        half_kernel,
        in_specs=[smem] * 2 + [vmem] * 6,
        out_shape=(
            jax.ShapeDtypeStruct((HALF, c_dim), F32),
            jax.ShapeDtypeStruct((count, c_dim), F32),
        ),
        scratch_shapes=gradient_scratch(n, c_dim),
        compiler_params=params(16),
        cost_estimate=pl.CostEstimate(
            flops=20 * n * count * c_dim, bytes_accessed=4 << 20, transcendentals=0
        ),
        name="half_step",
    )(core, blk, kern, got, eig, scale, targets, weights)


def step_kernel(
    core_ref,
    blk_ref,
    kern_ref,
    got_ref,
    eig_ref,
    scale_ref,
    targets_ref,
    base_ref,
    own_ref,
    pred_ref,
    out_ref,
    resid,
    head,
    other,
    new,
    sem,
    pred_sem,
):
    core = core_ref[0]
    own_copy = pltpu.make_async_copy(
        own_ref, pred_ref.at[pl.ds(pl.multiple_of(core * HALF, HALF), HALF)], pred_sem.at[0]
    )
    own_copy.start()
    step = scale_ref[:, LANES + 32 :]
    copies = []

    def add(rows, product):
        new[rows, :] = base_ref[rows, :] - step * product
        k = len(copies)
        copies.append(pltpu.make_async_copy(new.at[rows], out_ref.at[rows], sem.at[k]))
        copies[k].start()

    gradient(
        1 - core,
        blk_ref[0],
        kern_ref,
        got_ref,
        eig_ref,
        scale_ref,
        targets_ref,
        other,
        resid,
        head,
        128,
        add,
    )
    other_copy = pltpu.make_async_copy(
        other, pred_ref.at[pl.ds(pl.multiple_of((1 - core) * HALF, HALF), HALF)], pred_sem.at[1]
    )
    other_copy.start()
    own_copy.wait()
    for copy in copies:
        copy.wait()
    other_copy.wait()


def take_step(core, blk, kern, got, eig, scale, targets, base, own):
    n, count = kern.shape
    c_dim = base.shape[1]
    smem = pl.BlockSpec(memory_space=pltpu.SMEM)
    vmem = pl.BlockSpec(memory_space=pltpu.VMEM)
    hbm = pl.BlockSpec(memory_space=pltpu.HBM)
    return pl.pallas_call(
        step_kernel,
        in_specs=[smem] * 2 + [vmem] * 7,
        out_specs=[hbm] * 2,
        out_shape=(
            jax.ShapeDtypeStruct(targets.shape, F32),
            jax.ShapeDtypeStruct(base.shape, F32),
        ),
        scratch_shapes=gradient_scratch(n, c_dim)
        + [
            pltpu.VMEM((HALF, c_dim), F32),
            pltpu.VMEM(base.shape, F32),
            pltpu.SemaphoreType.DMA((8,)),
            pltpu.SemaphoreType.DMA((2,)),
        ],
        compiler_params=params(16),
        cost_estimate=pl.CostEstimate(
            flops=2 * n * count * c_dim, bytes_accessed=8 << 20, transcendentals=0
        ),
        name="take_step",
    )(core, blk, kern, got, eig, scale, targets, base, own)


def sq_norm(rows):
    return jnp.sum(rows.astype(F32) ** 2, axis=1) * scale_of(rows.shape[1])


def swap_cores(value):
    return lax.ppermute(value, "c", [(0, 1), (1, 0)])


def local(batch, targets, centers, weights, eigvec, eig_scale, step):
    core = lax.axis_index("c").reshape(1)
    sub = lax.axis_index(SUB_AXES).reshape(1)
    blk = lax.axis_index(BLK).reshape(1)
    n, d = BLOCKS * HALF, batch.shape[1]

    first = lax.all_to_all(fan(core, sub, blk, batch), BLK, 0, 0, tiled=True).reshape(n, d)
    first, held, to_split = lax.optimization_barrier((first, centers, weights))
    second = swap_cores(first)
    cs = sq_norm(held)[None, :]
    count, c_dim = weights.shape
    extra = (
        jax.ShapeDtypeStruct((3 * count, c_dim), BF16),
        jax.ShapeDtypeStruct((HALF, 2 * LANES), F32),
    )
    sent, kern_first, weights3, eig = terms(
        first_kernel, first, held, cs, to_split, eigvec, extra
    )
    kept, kern_second = terms(second_kernel, second, held, cs, weights3, eig)
    coded = code(kept, swap_cores(sent)).astype(F16)

    got = lax.all_to_all(coded, NEAR, 0, 0, tiled=True).astype(F32)
    partial = recode(got).astype(F16)
    partial = jnp.broadcast_to(partial[None], (FAR_SIZE,) + partial.shape)
    far = lax.all_to_all(partial, FAR, 0, 0, tiled=True).astype(F32)

    packed = pack(core, sub, blk, far, targets).astype(F16)
    got_second = lax.all_to_all(packed, NEAR, 0, 0, tiled=True)
    got_first = swap_cores(got_second)
    scale = jnp.concatenate([eig_scale, step])[None, :]
    own, base = half_step(
        core, blk, kern_second, got_second.astype(F32), eig, scale, targets, weights
    )
    return take_step(
        core, blk, kern_first, got_first.astype(F32), eig, scale, targets, base, own
    )


def solution(mesh):
    fine = Mesh(mesh.devices.reshape(2, 4, 4, 2, 2, 2), AXES)
    return jax.shard_map(
        local,
        mesh=fine,
        in_specs=(P(BLK, None), P(BLK, None), ALL, ALL, ALL, P(), P()),
        out_specs=(P(BLK, None), ALL),
        check_vma=False,
    )
```
